128 devices in a mesh: gx: 32 (over y, z, core), gy: 4 (over x).
Axes of the slice: x: 4, y: 4, z: 4, core: 2. Of those that a mesh axis runs over, the one named last changes fastest.
Arguments:
- beta: float32 [512, 256, 256], P('gx', 'gy'), may hold values from 0.25 to 4
- jump_rhs: float32 [262144], P(('gx', 'gy')), may hold values from -15 to 15
- stiffness: float32 [262144], P(('gx', 'gy')), may hold values from 0.1 to 1
- spread_weight: float32 [262144], P(('gx', 'gy')), may hold values from 0.5 to 1.5
- grid_owner: int32 [262144, 1], P(('gx', 'gy')), may hold values from 0 to 127; in each aligned block of 2048 rows (0 to 2047, 2048 to 4095, ...) at most 32 rows name the same one
- cell_index: int32 [262144], P(('gx', 'gy')), may hold values from 0 to 262143
- block_count: int32 [128], P(('gx', 'gy')), may hold values from 8 to 16, as said below
Outputs:
- solution: float32 [262144], P(('gx', 'gy'))
- residual: float32 [262144], P(('gx', 'gy'))
The draws below stay inside these ranges and needn't reach their ends.
Inputs may be any that keep to these rules, and one draw needn't show every extreme that they name: `grid_owner`: among the 2048 slots of each owner no device is named more than 32 times, and some device exactly 32 times. `cell_index`: cells are numbered with x slowest, then y, then z, inside the tile of 16 x 64 x 256 cells. `block_count`: slots in later blocks of an owner are padding; some owner has all 16 blocks live.
All inputs are finite; a program needn't handle non-finite values.
Results may differ from the reference program's by a relative error of at most 0.0003.
Values sent between devices are 32-bit elements; how exact they have to be, the bound alone decides.
A program may use at most 64 MiB of HBM per device.

```python
import math
import jax
import jax.numpy as jnp
import numpy as np

CX = 16
CY = 64
NZ = 256
NB_DEV = 16
BLOCK = 128
CHEB = 6
ITERS = 2
OWNERS = 128
P_DEV = 2048
CAP = 32
POINTS = 262144
NX = 512
NY = 256
N_GY = 4


def draw_jump_rhs(key, part):
    first, second = jax.random.split(jax.random.fold_in(key, 11))
    index = jnp.arange(POINTS)
    owner = index // P_DEV
    fraction = owner.astype(jnp.float32) / max(OWNERS - 1, 1)
    blocks = POINTS // BLOCK
    jitter = jax.random.uniform(second, (blocks,), jnp.float32, 0.0, 0.5)[index // BLOCK]
    values = jnp.clip(jax.random.normal(first, (POINTS,), jnp.float32), -3.0, 3.0)
    scale = 10.0 ** (0.5 * fraction + jitter) / 3.0
    return (values * scale).astype(jnp.float32)


def draw_block_count(key, part):
    first, second = jax.random.split(jax.random.fold_in(key, 7))
    lowest = max(NB_DEV // 2, 1)
    counts = jax.random.randint(first, (OWNERS,), lowest, NB_DEV + 1, dtype=jnp.int32)
    chosen = jax.random.randint(second, (), 0, OWNERS, dtype=jnp.int32)
    return jnp.where(jnp.arange(OWNERS) == chosen, NB_DEV, counts).astype(jnp.int32)


def touch_ends(drawn, own_key, least, largest):
    index_at = [jax.random.randint(jax.random.fold_in(own_key, axis), (), 0, length) for axis, length in enumerate(drawn.shape)]
    main_axis = drawn.shape.index(max(drawn.shape))
    neighbour = index_at[:main_axis] + [(index_at[main_axis] + 1) % drawn.shape[main_axis]] + index_at[main_axis + 1:]
    return drawn.at[tuple(index_at)].set(least).at[tuple(neighbour)].set(largest)


def levels(stream_key, dims, cuts, smallest, largest):
    factor_of = 1.0
    for dim, parts in cuts:
        steps = jax.random.uniform(jax.random.fold_in(jax.random.fold_in(stream_key, 6), dim), (parts,), jnp.float32, smallest / len(cuts), largest / len(cuts))
        factor_of = factor_of * jnp.repeat(jnp.exp(steps), dims[dim] // parts).reshape((-1,) + (1,) * (len(dims) - 1 - dim))
    return factor_of


def assign_block(key, own, number, rows, number_of, top, bound, slope):
    sequence = jax.random.permutation(key, number_of)
    heavy_load, common = shares(number_of, rows * top, bound, slope, True), shares(number_of, rows * top, bound, slope, False)
    places = jnp.arange(number_of)

    def named(sizes, offset_by):
        used = int((sizes > 0).sum())
        fixed = max(1, used // 4)
        passed = fixed + (places - fixed + offset_by * (used - fixed)) % max(1, number_of - fixed)
        return jnp.zeros((number_of,), jnp.int32).at[sequence[jnp.where(places < fixed, places, passed)]].set(jnp.asarray(sizes, jnp.int32))

    sizes = jnp.where(number % 4 == 0, named(heavy_load, number // 4), named(common, number - number // 4 - 1))
    mixed = jax.random.permutation(jax.random.fold_in(own, 3), number_of)
    source_of, taker = mixed[0:number_of // 2 * 2:2], mixed[1:number_of // 2 * 2:2]
    slack = jnp.minimum(sizes[source_of] - 1, bound - sizes[taker]) // 2
    slack = jnp.where((source_of == sequence[0]) | (taker == sequence[0]) | (sizes[taker] == 0), 0, jnp.maximum(slack, 0))
    passed = jax.random.randint(jax.random.fold_in(own, 4), (number_of // 2,), 0, 1 << 20) % (slack + 1)
    sizes = sizes.at[source_of].add(-passed).at[taker].add(passed)
    members = jnp.searchsorted(jnp.cumsum(sizes), jnp.arange(rows * top), side="right").astype(jnp.int32)
    listing = members.reshape(top, rows).T
    listing = listing[jax.random.permutation(jax.random.fold_in(own, 1), rows)]
    offset_by = jax.random.randint(jax.random.fold_in(own, 2), (rows, 1), 0, top)
    return jnp.take_along_axis(listing, (jnp.arange(top)[None, :] + offset_by) % top, axis=1)


def shares(number_of, total, limit, skew, full):
    loads = [(1 << 20) // math.isqrt(standing ** skew) + 1 for standing in range(1, number_of + 1)]
    largest = limit if full else min(limit, max(-(-total // number_of), total * loads[0] // sum(loads)))
    least = 1 if total - largest >= number_of - 1 else 0
    given, spare = [largest] + [least] * (number_of - 1), total - largest - least * (number_of - 1)
    while spare > 0:
        free = [i for i in range(1, number_of) if given[i] < largest] or [i for i in range(1, number_of) if given[i] < limit]
        pool, remaining = sum([loads[i] for i in free]), spare
        for i in free:
            addition = min(limit - given[i], max(1, remaining * loads[i] // pool), spare)
            given[i] = given[i] + addition
            spare = spare - addition
    return np.array(given)


def setup_inputs(seed: int = 0) -> dict:
    streams_of = jax.random.split(jax.random.key(seed), 8)
    beta = jnp.clip(jnp.exp(math.log(4.0) - 2.7725887 * jax.random.uniform(streams_of[0], (NX, NY, NZ), jnp.float32) ** levels(streams_of[0], (NX, NY, NZ), ((0, 32), (1, 4)), -0.2, 0.2)), 0.25, 4.0)
    jump_rhs = draw_jump_rhs(jax.random.fold_in(streams_of[7], 71), 0)
    stiffness = jnp.clip(jnp.exp(math.log(1.0) - 2.3025851 * jax.random.uniform(streams_of[2], (POINTS,), jnp.float32) ** levels(streams_of[2], (POINTS,), ((0, 128),), -0.2, 0.2)), 0.1, 1.0)
    spread_weight = jnp.clip(0.5 + 1.0 * jax.random.uniform(streams_of[3], (POINTS,), jnp.float32) ** levels(streams_of[3], (POINTS,), ((0, 128),), -0.2, 0.2), 0.5, 1.5)
    grid_owner_keys = jax.random.split(jax.random.fold_in(streams_of[4], 1), POINTS // P_DEV)
    grid_owner_turns = jax.random.permutation(jax.random.fold_in(streams_of[4], 3), POINTS // P_DEV)
    grid_owner = jax.vmap(lambda own, number: assign_block(jax.random.fold_in(streams_of[4], 2), own, number, P_DEV, OWNERS, 1, CAP, 2))(grid_owner_keys, grid_owner_turns).reshape((POINTS, 1))
    cell_index = touch_ends(jax.random.randint(streams_of[5], (POINTS,), 0, CX * CY * NZ), jax.random.fold_in(streams_of[5], 1), 0, (CX * CY * NZ) - 1).astype(jnp.int32)
    block_count = draw_block_count(jax.random.fold_in(streams_of[7], 71), 0)
    return {"beta": beta, "jump_rhs": jump_rhs, "stiffness": stiffness, "spread_weight": spread_weight, "grid_owner": grid_owner, "cell_index": cell_index, "block_count": block_count}


SHIFT = 0.01
THETA = 1.025
DELTA = 0.975
SIGMA = THETA / DELTA
EPS = 1e-06

def harmonic(left, right):
    total = left + right
    return 2.0 * left * right / jnp.where(total > 0, total, 1.0)

def faces(beta_pad):
    padded = jnp.pad(beta_pad, ((0, 0), (0, 0), (1, 1)))
    coef_x = harmonic(padded[:-1, 1:-1, 1:-1], padded[1:, 1:-1, 1:-1])
    coef_y = harmonic(padded[1:-1, :-1, 1:-1], padded[1:-1, 1:, 1:-1])
    coef_z = harmonic(padded[1:-1, 1:-1, :-1], padded[1:-1, 1:-1, 1:])
    diagonal = SHIFT + coef_x[:-1] + coef_x[1:] + coef_y[:, :-1] + coef_y[:, 1:] + coef_z[:, :, :-1] + coef_z[:, :, 1:]
    return (coef_x, coef_y, coef_z, diagonal)

def operate(field_pad, coef_x, coef_y, coef_z, diagonal):
    padded = jnp.pad(field_pad, ((0, 0), (0, 0), (1, 1)))
    centre = padded[1:-1, 1:-1, 1:-1]
    beside = coef_x[1:] * padded[2:, 1:-1, 1:-1] + coef_x[:-1] * padded[:-2, 1:-1, 1:-1]
    beside = beside + coef_y[:, 1:] * padded[1:-1, 2:, 1:-1] + coef_y[:, :-1] * padded[1:-1, :-2, 1:-1]
    beside = beside + coef_z[:, :, 1:] * padded[1:-1, 1:-1, 2:] + coef_z[:, :, :-1] * padded[1:-1, 1:-1, :-2]
    return diagonal * centre - beside

def chebyshev(source, coefs):
    coef_x, coef_y, coef_z, diagonal = coefs
    ratio = 1.0 / SIGMA
    update = source / (THETA * diagonal)
    field = update
    for sweep in range(CHEB - 1):
        image = operate(jnp.pad(field, ((1, 1), (1, 1), (0, 0))), coef_x, coef_y, coef_z, diagonal)
        ratio_next = 1.0 / (2.0 * SIGMA - ratio)
        update = ratio_next * ratio * update + 2.0 * ratio_next / DELTA * (source - image) / diagonal
        field = field + update
        ratio = ratio_next
    return field

def least_squares(start, columns):
    count = len(columns)
    targets = [start] + [start * 0.0 for unused in range(count)]
    cosines = []
    sines = []
    upper = []
    for outer in range(count):
        column = list(columns[outer])
        for inner in range(outer):
            first = cosines[inner] * column[inner] + sines[inner] * column[inner + 1]
            second = -sines[inner] * column[inner] + cosines[inner] * column[inner + 1]
            column[inner] = first
            column[inner + 1] = second
        radius = jnp.sqrt(column[outer] * column[outer] + column[outer + 1] * column[outer + 1])
        cosine = column[outer] / radius
        sine = column[outer + 1] / radius
        column[outer] = radius
        targets[outer + 1] = -sine * targets[outer]
        targets[outer] = cosine * targets[outer]
        cosines.append(cosine)
        sines.append(sine)
        upper.append(column)
    coeffs = [None] * count
    for outer in reversed(range(count)):
        total = targets[outer]
        for later in range(outer + 1, count):
            total = total - upper[later][outer] * coeffs[later]
        coeffs[outer] = total / upper[outer][outer]
    return coeffs

def reference(beta, jump_rhs, stiffness, spread_weight, grid_owner, cell_index, block_count):
    index = jnp.arange(POINTS, dtype=jnp.int32)
    owner = index // P_DEV
    live = index % P_DEV // BLOCK < block_count[owner]
    target = grid_owner[:, 0]
    cell_x = target // N_GY * CX + cell_index // (CY * NZ)
    cell_y = target % N_GY * CY + cell_index // NZ % CY
    cell_z = cell_index % NZ
    coefs = faces(jnp.pad(beta, ((1, 1), (1, 1), (0, 0))))

    def apply_schur(vector):
        source = jnp.zeros((NX, NY, NZ), jnp.float32).at[cell_x, cell_y, cell_z].add(spread_weight * vector)
        field = chebyshev(source, coefs)
        return jnp.where(live, stiffness * vector + spread_weight * field[cell_x, cell_y, cell_z], 0.0)
    rhs = jnp.where(live, jump_rhs, 0.0)
    start = jnp.sqrt(jnp.sum(rhs * rhs) + EPS)
    basis = [rhs / start]
    images = []
    columns = []
    for step in range(ITERS):
        image = apply_schur(basis[step])
        images.append(image)
        remainder = image
        column = []
        for vector in basis:
            height = jnp.sum(remainder * vector)
            remainder = remainder - height * vector
            column.append(height)
        norm = jnp.sqrt(jnp.sum(remainder * remainder) + EPS)
        column.append(norm)
        columns.append(column)
        basis.append(remainder / norm)
    coeffs = least_squares(start, columns)
    solution = jnp.zeros_like(rhs)
    residual = rhs
    for step in range(ITERS):
        solution = solution + coeffs[step] * basis[step]
        residual = residual - coeffs[step] * images[step]
    return (solution, residual)
```

```python
import functools

import jax
import jax.numpy as jnp
from jax import lax
from jax.experimental import pallas as pl
from jax.experimental.pallas import tpu as pltpu
from jax.sharding import PartitionSpec as P

CHEB = 6
SHIFT = 0.01
THETA = 1.025
DELTA = 0.975
SIGMA = THETA / DELTA
EPS = 1e-06
LANES = 128
PAD = 8
MESH = pl.DeviceIdType.MESH
F32 = jnp.float32
BF16 = jnp.bfloat16
CHUNK = 512


def sweep_factors():
    factors = []
    ratio = 1.0 / SIGMA
    for _ in range(CHEB - 1):
        ratio_next = 1.0 / (2.0 * SIGMA - ratio)
        factors.append((ratio_next * ratio, 2.0 * ratio_next / DELTA))
        ratio = ratio_next
    return factors


def least_squares(start, columns):
    count = len(columns)
    targets = [start] + [start * 0.0 for unused in range(count)]
    cosines = []
    sines = []
    upper = []
    for outer in range(count):
        column = list(columns[outer])
        for inner in range(outer):
            first = cosines[inner] * column[inner] + sines[inner] * column[inner + 1]
            second = -sines[inner] * column[inner] + cosines[inner] * column[inner + 1]
            column[inner] = first
            column[inner + 1] = second
        radius = jnp.sqrt(column[outer] * column[outer] + column[outer + 1] * column[outer + 1])
        cosine = column[outer] / radius
        sine = column[outer + 1] / radius
        column[outer] = radius
        targets[outer + 1] = -sine * targets[outer]
        targets[outer] = cosine * targets[outer]
        cosines.append(cosine)
        sines.append(sine)
        upper.append(column)
    coeffs = [None] * count
    for outer in reversed(range(count)):
        total = targets[outer]
        for later in range(outer + 1, count):
            total = total - upper[later][outer] * coeffs[later]
        coeffs[outer] = total / upper[outer][outer]
    return coeffs


def halves(x):
    high = x.astype(BF16)
    low = (x - high.astype(F32)).astype(BF16)
    return high, low


def nt_dot(a, b):
    return lax.dot_general(a, b, (((1,), (1,)), ((), ())), preferred_element_type=F32)


def nn_dot(a, b):
    return lax.dot_general(a, b, (((1,), (0,)), ((), ())), preferred_element_type=F32)


def total(x):
    return jnp.sum(jnp.sum(x, axis=0, keepdims=True), axis=1, keepdims=True)


def pack_row(values):
    lane = lax.broadcasted_iota(jnp.int32, (1, LANES), 1)
    row = jnp.zeros((1, LANES), F32)
    for at, value in enumerate(values):
        row = jnp.where(lane == at, value, row)
    return row


def unpack_row(row, count):
    lane = lax.broadcasted_iota(jnp.int32, (1, LANES), 1)
    return [
        jnp.sum(jnp.where(lane == at, row, 0.0), axis=1, keepdims=True) for at in range(count)
    ]


def kernel(
    n_gx,
    n_gy,
    beta,
    jump,
    stiff,
    weight,
    owner,
    cell,
    count,
    sol,
    res,
    t_one,
    l_one,
    target,
    lanes_at,
    u,
    d,
    g,
    invd,
    axl,
    axh,
    ayl,
    ayh,
    azl,
    azh,
    acc,
    field_t,
    c_one,
    z_at,
    slot_val,
    picked,
    sampled,
    y_send,
    y_recv,
    fa_send,
    fa_recv,
    fb_send,
    fb_recv,
    rb_send,
    rb_recv,
    ra_send,
    ra_recv,
    pb_send,
    pb_recv,
    pa_send,
    pa_recv,
    fa_ss,
    fa_rs,
    fb_ss,
    fb_rs,
    rb_ss,
    rb_rs,
    ra_ss,
    ra_rs,
    p_ss,
    p_rs,
    x_ss,
    x_rs,
    y_ss,
    y_rs,
):
    me_x = lax.axis_index("gx")
    me_y = lax.axis_index("gy")
    size_x, size_y, size_z = beta.shape
    rows = jump.shape[0]
    points = rows * LANES
    owners = n_gx * n_gy
    cap = LANES // n_gy
    slots = n_gx * LANES
    columns = size_x * size_y
    chunk = min(CHUNK, slots)
    lane8 = lax.broadcasted_iota(jnp.int32, (PAD, LANES), 1)

    def at_gx(shift):
        return {"gx": lax.rem(me_x + shift + n_gx, n_gx), "gy": me_y}

    def at_gy(shift):
        return {"gx": me_x, "gy": lax.rem(me_y + shift + n_gy, n_gy)}

    for p in range(2):
        for x in (0, size_x + 1):
            u[p, x] = jnp.zeros(u.shape[2:], F32)
    zero_tile = jnp.zeros((2, PAD, LANES), F32)

    def clear(x, _):
        for p in range(2):
            u[p, x, :, 0:PAD, :] = zero_tile
            u[p, x, :, PAD + size_y : 2 * PAD + size_y, :] = zero_tile
        return 0

    lax.fori_loop(1, size_x + 1, clear, 0)

    barrier = pltpu.get_barrier_semaphore()

    def greet_x(k, _):
        pl.semaphore_signal(barrier, inc=1, device_id=at_gx(k), device_id_type=MESH)
        return 0

    def greet_y(k, _):
        pl.semaphore_signal(barrier, inc=1, device_id=at_gy(k), device_id_type=MESH)
        return 0

    lax.fori_loop(1, n_gx, greet_x, 0)
    lax.fori_loop(1, n_gy, greet_y, 0)

    def gx_copy(src, dst, send, recv, k, sign):
        return pltpu.make_async_remote_copy(
            src_ref=src,
            dst_ref=dst,
            send_sem=send,
            recv_sem=recv,
            device_id=at_gx(sign * k),
            device_id_type=MESH,
        )

    def gy_copy(src, dst, send, recv, k, sign):
        return pltpu.make_async_remote_copy(
            src_ref=src,
            dst_ref=dst,
            send_sem=send,
            recv_sem=recv,
            device_id=at_gy(sign * k),
            device_id_type=MESH,
        )

    def wait_for(ref, sem):
        pltpu.make_async_copy(ref, ref, sem).wait()

    def send_gx(src, dst, send, recv, sign):
        def body(k, _):
            gx_copy(src.at[k], dst.at[k], send, recv, k, sign).start()
            return 0

        lax.fori_loop(1, n_gx, body, 0)

    def halo_copies(p, which):
        rows_in = pl.ds(PAD, size_y)
        copies = (
            (
                me_x > 0,
                lambda: gx_copy(
                    u.at[p, 1, :, rows_in, :],
                    u.at[p, size_x + 1, :, rows_in, :],
                    x_ss.at[p, 0],
                    x_rs.at[p, 1],
                    1,
                    -1,
                ),
            ),
            (
                me_x < n_gx - 1,
                lambda: gx_copy(
                    u.at[p, size_x, :, rows_in, :],
                    u.at[p, 0, :, rows_in, :],
                    x_ss.at[p, 1],
                    x_rs.at[p, 0],
                    1,
                    1,
                ),
            ),
            (
                me_y > 0,
                lambda: gy_copy(
                    y_send.at[p, 0], y_recv.at[p, 1], y_ss.at[p, 0], y_rs.at[p, 1], 1, -1
                ),
            ),
            (
                me_y < n_gy - 1,
                lambda: gy_copy(
                    y_send.at[p, 1], y_recv.at[p, 0], y_ss.at[p, 1], y_rs.at[p, 0], 1, 1
                ),
            ),
        )
        return [copies[i] for i in which]

    def halo_send_x(p):
        for on, copy in halo_copies(p, (0, 1)):
            pl.when(on)(lambda: copy().start())

    def halo_send_y(p):
        def pack(x, _):
            for h in range(2):
                y_send[p, 0, x, h] = u[p, x + 1, h, PAD : PAD + 1, :]
                y_send[p, 1, x, h] = u[p, x + 1, h, PAD + size_y - 1 : PAD + size_y, :]
            return 0

        lax.fori_loop(0, size_x, pack, 0)
        for on, copy in halo_copies(p, (2, 3)):
            pl.when(on)(lambda: copy().start())

    def halo_wait_sent(p):
        for on, copy in halo_copies(p, range(4)):
            pl.when(on)(lambda: copy().wait_send())

    def halo_wait(p):
        (_, down_x), (_, up_x), (_, down_y), (_, up_y) = halo_copies(p, range(4))
        pl.when(me_x < n_gx - 1)(lambda: down_x().wait_recv())
        pl.when(me_x > 0)(lambda: up_x().wait_recv())

        @pl.when(me_y < n_gy - 1)
        def _():
            down_y().wait_recv()

            def unpack(x, _):
                for h in range(2):
                    u[p, x + 1, h, PAD + size_y : PAD + size_y + 1, :] = y_recv[p, 1, x, h]
                return 0

            lax.fori_loop(0, size_x, unpack, 0)

        @pl.when(me_y > 0)
        def _():
            up_y().wait_recv()

            def unpack(x, _):
                for h in range(2):
                    u[p, x + 1, h, PAD - 1 : PAD, :] = y_recv[p, 0, x, h]
                return 0

            lax.fori_loop(0, size_x, unpack, 0)

    shift_gy = n_gy.bit_length() - 1
    own = owner[...]
    target[...] = ((own & (n_gy - 1)) - me_y & (n_gy - 1)) * n_gx + (
        (own >> shift_gy) - me_x & (n_gx - 1)
    )
    iota_t = lax.broadcasted_iota(jnp.int32, (owners, LANES), 0)
    iota_l = lax.broadcasted_iota(jnp.int32, (LANES, LANES), 0)
    above = lax.broadcasted_iota(jnp.int32, (LANES, 2 * LANES), 1)
    below = lax.broadcasted_iota(jnp.int32, (LANES, 2 * LANES), 0)
    counter = ((below < above) | (above >= LANES)).astype(BF16)
    offset = jnp.zeros((owners, LANES), F32)
    for j in range(rows):
        hit = target[j : j + 1, :] == iota_t
        hit_f = jnp.where(hit, 1.0, 0.0)
        hit_b = hit_f.astype(BF16)
        t_one[:, j * LANES : (j + 1) * LANES] = hit_b
        both = nn_dot(hit_b, counter)
        rank = jnp.sum(hit_f * (both[:, :LANES] + offset), axis=0, keepdims=True)
        offset = offset + both[:, LANES:]
        lane_of = rank.astype(jnp.int32) + me_y * cap
        l_one[:, j * LANES : (j + 1) * LANES] = jnp.where(lane_of == iota_l, 1.0, 0.0).astype(BF16)

    def to_rows(vector, row_of):
        out = jnp.zeros((owners, LANES), F32)
        for j in range(rows):
            cols = slice(j * LANES, (j + 1) * LANES)
            for part in row_of(vector[j : j + 1, :]):
                spread = t_one[:, cols] * part
                out = out + nt_dot(spread, l_one[:, cols])
        return out

    def split_index(row):
        low = (row & (2 * LANES - 1)) + 1
        middle = (row >> 8) & (2 * LANES - 1)
        high = row >> 16
        return [
            x.astype(F32).astype(BF16) for x in (low, middle * 256, high * 65536)
        ]

    def forward_a(f, first, second):
        for k in range(n_gy):
            fa_send[f, k, 0:n_gx, :] = first[k * n_gx : (k + 1) * n_gx, :]
            fa_send[f, k, n_gx : 2 * n_gx, :] = second[k]
        for k in range(1, n_gy):
            gy_copy(fa_send.at[f, k], fa_recv.at[f, k], fa_ss.at[f], fa_rs.at[f], k, 1).start()

    def forward_b(f):
        wait_for(fa_recv.at[f, pl.ds(1, n_gy - 1)], fa_rs.at[f])
        both = fa_send[f, 0]
        for k in range(1, n_gy):
            both = both + fa_recv[f, k]
        for k in range(n_gx):
            fb_send[f, k, 0:1, :] = both[k : k + 1, :]
            fb_send[f, k, 1:2, :] = both[n_gx + k : n_gx + k + 1, :]
        send_gx(fb_send.at[f], fb_recv.at[f], fb_ss.at[f], fb_rs.at[f], 1)
        fb_recv[f, 0] = fb_send[f, 0]

    def forward_c(f):
        wait_for(fb_recv.at[f, pl.ds(1, n_gx - 1)], fb_rs.at[f])
        return fb_recv[f, :, 0, :], fb_recv[f, :, 1, :]

    def back_a(f, second):
        for k in range(n_gx):
            rb_send[f, k, 0:1, :] = picked[k : k + 1, :]
            rb_send[f, k, 1:2, :] = second
        send_gx(rb_send.at[f], rb_recv.at[f], rb_ss.at[f], rb_rs.at[f], -1)
        rb_recv[f, 0] = rb_send[f, 0]

    def back_b(f):
        wait_for(rb_recv.at[f, pl.ds(1, n_gx - 1)], rb_rs.at[f])
        ra_send[f, 0:n_gx, :] = rb_recv[f, :, 0, :]
        ra_send[f, n_gx : 2 * n_gx, :] = rb_recv[f, :, 1, :]
        for k in range(1, n_gy):
            gy_copy(ra_send.at[f], ra_recv.at[f, k], ra_ss.at[f], ra_rs.at[f], k, -1).start()

    def back_c(f):
        wait_for(ra_recv.at[f, pl.ds(1, n_gy - 1)], ra_rs.at[f])
        blocks = [ra_send[f]] + [ra_recv[f, k] for k in range(1, n_gy)]
        high, low = halves(jnp.concatenate([b[0:n_gx, :] for b in blocks], axis=0))
        rest = blocks[0][n_gx:, :]
        for b in blocks[1:]:
            rest = rest + b[n_gx:, :]
        for j in range(rows):
            cols = slice(j * LANES, (j + 1) * LANES)
            lanes = l_one[:, cols]
            found = nn_dot(high, lanes) + nn_dot(low, lanes)
            sampled[j : j + 1, :] = jnp.sum(
                found * t_one[:, cols].astype(F32), axis=0, keepdims=True
            )
        return sampled[...], jnp.sum(rest, axis=0, keepdims=True)

    live = lax.broadcasted_iota(jnp.int32, (rows, LANES), 0) < count[...]
    rhs = jnp.where(live, jump[...], 0.0)
    sw = weight[...]
    cells = cell[...]
    index_rows = to_rows(cells, split_index)
    value_rows = to_rows(sw * rhs, halves)
    pl.semaphore_wait(barrier, n_gx + n_gy - 2)
    forward_a(0, index_rows, [value_rows[k * n_gx : (k + 1) * n_gx, :] for k in range(n_gy)])

    def place(x, _):
        for h in range(2):
            u[1, x + 1, h, PAD : PAD + size_y, :] = beta[x, :, h * LANES : (h + 1) * LANES]
        return 0

    lax.fori_loop(0, size_x, place, 0)
    halo_send_x(1)
    halo_send_y(1)
    forward_b(0)

    def rows_at(ref, p, x, h, start, n):
        return ref[p, x, h, pl.ds(start, n), :]

    def z_sides(low, high, lane):
        low_up, high_up = pltpu.roll(low, 1, 1), pltpu.roll(high, 1, 1)
        low_dn, high_dn = pltpu.roll(low, LANES - 1, 1), pltpu.roll(high, LANES - 1, 1)
        return (
            (low_up, jnp.where(lane == 0, low_up, high_up)),
            (jnp.where(lane == LANES - 1, high_dn, low_dn), high_dn),
        )

    def harmonic(a, b):
        return 2.0 * a * b / (a + b)

    halo_wait(1)

    def coefficients(step, _):
        x = step // (size_y // PAD)
        y = (step % (size_y // PAD)) * PAD
        centre = [rows_at(u, 1, x + 1, h, y + PAD, PAD) for h in range(2)]
        before, after = z_sides(centre[0], centre[1], lane8)
        for h in range(2):
            c = centre[h]
            kxl = harmonic(c, rows_at(u, 1, x, h, y + PAD, PAD))
            kxh = harmonic(c, rows_at(u, 1, x + 2, h, y + PAD, PAD))
            kyl = harmonic(c, rows_at(u, 1, x + 1, h, y + PAD - 1, PAD))
            kyh = harmonic(c, rows_at(u, 1, x + 1, h, y + PAD + 1, PAD))
            kzl = harmonic(c, before[h])
            kzh = harmonic(c, after[h])
            if h == 0:
                kzl = jnp.where(lane8 == 0, 0.0, kzl)
            else:
                kzh = jnp.where(lane8 == LANES - 1, 0.0, kzh)
            inverse = 1.0 / (SHIFT + kxl + kxh + kyl + kyh + kzl + kzh)
            at = (x, h, pl.ds(y, PAD), slice(None))
            invd[at] = inverse
            axl[at] = kxl * inverse
            axh[at] = kxh * inverse
            ayl[at] = kyl * inverse
            ayh[at] = kyh * inverse
            azl[at] = kzl * inverse
            azh[at] = kzh * inverse
        return 0

    lax.fori_loop(0, size_x * (size_y // PAD), coefficients, 0)
    halo_wait_sent(1)

    index, values = forward_c(0)
    index = index.astype(jnp.int32) - 1
    z_at[...] = jnp.where(index < 0, -1, index & (size_z - 1))
    slot_val[...] = index >> 8
    iota_c = lax.broadcasted_iota(jnp.int32, (columns, LANES), 0)
    per = chunk // LANES

    def column_table(j, _):
        row = slot_val[pl.ds(j, 1), :]
        c_one[j] = jnp.where(row == iota_c, 1.0, 0.0).astype(BF16)
        return 0

    lax.fori_loop(0, n_gx, column_table, 0)
    iota_z = lax.broadcasted_iota(jnp.int32, (size_z, LANES), 0)

    def spread_grid(values):
        picked[...] = values
        acc[...] = jnp.zeros_like(acc)

        def body(i, _):
            high_parts, low_parts, col_parts = [], [], []
            for q in range(per):
                j = i * per + q
                row = picked[pl.ds(j, 1), :]
                hit = z_at[pl.ds(j, 1), :] == iota_z
                high = row.astype(BF16).astype(F32)
                high_parts.append(jnp.where(hit, high, 0.0).astype(BF16))
                low_parts.append(jnp.where(hit, row - high, 0.0).astype(BF16))
                col_parts.append(c_one[j])
            cols = jnp.concatenate(col_parts, axis=1)
            acc[...] += nt_dot(cols, jnp.concatenate(high_parts, axis=1)) + nt_dot(
                cols, jnp.concatenate(low_parts, axis=1)
            )
            return 0

        lax.fori_loop(0, slots // chunk, body, 0)

    def sample_grid(p):
        def turn(x, _):
            for h in range(2):
                high, low = halves(u[p, x + 1, h, PAD : PAD + size_y, :].T)
                field_t[x, h * LANES : (h + 1) * LANES, :] = high
                field_t[x, size_z + h * LANES : size_z + (h + 1) * LANES, :] = low
            return 0

        lax.fori_loop(0, size_x, turn, 0)
        whole = jnp.concatenate([field_t[x] for x in range(size_x)], axis=1)

        def body(i, _):
            found = nn_dot(
                whole, jnp.concatenate([c_one[i * per + q] for q in range(per)], axis=1)
            )
            for q in range(per):
                j = i * per + q
                hit = z_at[pl.ds(j, 1), :] == iota_z
                cols = slice(q * LANES, (q + 1) * LANES)
                both = found[:size_z, cols] + found[size_z:, cols]
                picked[pl.ds(j, 1), :] = jnp.sum(
                    jnp.where(hit, both, 0.0), axis=0, keepdims=True
                )
            return 0

        lax.fori_loop(0, slots // chunk, body, 0)

    def relax(p, x, y, n, first, second):
        lane = lax.broadcasted_iota(jnp.int32, (n, LANES), 1)
        centre = [rows_at(u, p, x + 1, h, y + PAD, n) for h in range(2)]
        before, after = z_sides(centre[0], centre[1], lane)
        for h in range(2):
            at = (x, h, pl.ds(y, n), slice(None))
            image = g[at] - centre[h]
            image += axl[at] * rows_at(u, p, x, h, y + PAD, n)
            image += axh[at] * rows_at(u, p, x + 2, h, y + PAD, n)
            image += ayl[at] * rows_at(u, p, x + 1, h, y + PAD - 1, n)
            image += ayh[at] * rows_at(u, p, x + 1, h, y + PAD + 1, n)
            image += azl[at] * before[h] + azh[at] * after[h]
            update = first * d[at] + second * image
            d[at] = update
            u[1 - p, x + 1, h, pl.ds(y + PAD, n), :] = centre[h] + update

    tiles = size_y // PAD

    def pressure():
        def begin(x, _):
            for h in range(2):
                source = acc[pl.ds(x * size_y, size_y), h * LANES : (h + 1) * LANES]
                scaled = source * invd[x, h]
                g[x, h] = scaled
                scaled = scaled * (1.0 / THETA)
                d[x, h] = scaled
                u[0, x + 1, h, PAD : PAD + size_y, :] = scaled
            return 0

        lax.fori_loop(0, size_x, begin, 0)
        halo_send_x(0)
        halo_send_y(0)
        for step, (first, second) in enumerate(sweep_factors()):
            p = step % 2
            last = step == CHEB - 2
            halo_wait(p)
            if step > 0:
                halo_wait_sent(1 - p)

            def side(i, _):
                x = lax.rem(i, 2) * (size_x - 1)
                relax(p, x, (i // 2) * PAD, PAD, first, second)
                return 0

            lax.fori_loop(0, 2 * tiles, side, 0)
            if not last:
                halo_send_x(1 - p)

            def edge(x, _):
                relax(p, x, 0 * x, PAD, first, second)
                relax(p, x, 0 * x + (size_y - PAD), PAD, first, second)
                return 0

            lax.fori_loop(1, size_x - 1, edge, 0)
            if not last:
                halo_send_y(1 - p)

            def inner(i, _):
                x = 1 + i // (tiles - 2)
                y = (1 + lax.rem(i, tiles - 2)) * PAD
                relax(p, x, y, PAD, first, second)
                return 0

            lax.fori_loop(0, (size_x - 2) * (tiles - 2), inner, 0)
        halo_wait_sent((CHEB - 2) % 2)
        return (CHEB - 1) % 2

    zero_row = jnp.zeros((1, LANES), F32)
    spread_grid(values)
    sample_grid(pressure())
    back_a(0, zero_row)
    back_b(0)
    got, _ = back_c(0)
    steady = stiff[...]
    image_1 = jnp.where(live, steady * rhs + sw * got, 0.0)

    partial = pack_row([total(rhs * rhs), total(rhs * image_1), total(image_1 * image_1)])
    partial_rows = jnp.broadcast_to(partial, (n_gx, LANES))
    forward_a(1, to_rows(sw * image_1, halves), [partial_rows] * n_gy)
    forward_b(1)
    values, sums = forward_c(1)
    sum_bb, sum_ab, _ = unpack_row(jnp.sum(sums, axis=0, keepdims=True), 3)
    start = jnp.sqrt(sum_bb + EPS)
    scale = 1.0 / start
    v_1 = rhs * scale
    w_1 = image_1 * scale
    h_11 = sum_ab * scale * scale
    rest_1 = w_1 - h_11 * v_1
    spread_grid(values)
    sample_grid(pressure())
    back_a(1, pack_row([total(rest_1 * rest_1)]))
    back_b(1)
    got, sums = back_c(1)
    image_2 = jnp.where(live, steady * image_1 + sw * got, 0.0)
    h_21 = jnp.sqrt(unpack_row(sums, 1)[0] + EPS)
    v_2 = rest_1 / h_21
    w_2 = (image_2 * scale - h_11 * w_1) / h_21

    partial = pack_row(
        [total(w_2 * v_1), total(w_2 * v_2), total(w_2 * w_2), total(v_1 * v_1), total(v_1 * v_2),
         total(v_2 * v_2)]
    )
    pb_send[...] = jnp.broadcast_to(partial, pb_send.shape)

    def spill(k, _):
        gx_copy(pb_send, pb_recv.at[k], p_ss.at[0], p_rs.at[0], k, 1).start()
        return 0

    lax.fori_loop(1, n_gx, spill, 0)
    pb_recv[0] = pb_send[...]
    wait_for(pb_recv.at[pl.ds(1, n_gx - 1)], p_rs.at[0])
    pa_send[...] = jnp.sum(pb_recv[...], axis=0)
    for k in range(1, n_gy):
        gy_copy(pa_send, pa_recv.at[k], p_ss.at[1], p_rs.at[1], k, 1).start()
    pa_recv[0] = pa_send[...]
    wait_for(pa_recv.at[pl.ds(1, n_gy - 1)], p_rs.at[1])
    sums = jnp.sum(pa_recv[...], axis=0)[0:1, :]
    w2v1, w2v2, w2w2, v1v1, v1v2, v2v2 = unpack_row(sums, 6)
    h_12 = w2v1
    h_22 = w2v2 - h_12 * v1v2
    square = (
        w2w2
        + h_12 * h_12 * v1v1
        + h_22 * h_22 * v2v2
        - 2.0 * h_12 * w2v1
        - 2.0 * h_22 * w2v2
        + 2.0 * h_12 * h_22 * v1v2
    )
    h_32 = jnp.sqrt(jnp.maximum(square, 0.0) + EPS)
    y_1, y_2 = least_squares(start, [[h_11, h_21], [h_12, h_22, h_32]])
    sol[...] = y_1 * v_1 + y_2 * v_2
    res[...] = rhs - y_1 * w_1 - y_2 * w_2

    for f in range(2):
        for k in range(1, n_gy):
            gy_copy(fa_send.at[f, k], fa_recv.at[f, k], fa_ss.at[f], fa_rs.at[f], k, 1).wait_send()
            gy_copy(ra_send.at[f], ra_recv.at[f, k], ra_ss.at[f], ra_rs.at[f], k, -1).wait_send()
        wait_for(fb_send.at[f, pl.ds(1, n_gx - 1)], fb_ss.at[f])
        wait_for(rb_send.at[f, pl.ds(1, n_gx - 1)], rb_ss.at[f])
    wait_for(pb_recv.at[pl.ds(1, n_gx - 1)], p_ss.at[0])
    wait_for(pa_recv.at[pl.ds(1, n_gy - 1)], p_ss.at[1])


def on_device(n_gx, n_gy, beta, jump, stiff, weight, owner, cell, count):
    size_x, size_y, size_z = beta.shape
    points = jump.shape[0]
    rows = points // LANES
    owners = n_gx * n_gy
    columns = size_x * size_y
    tile = (size_x, 2, size_y, LANES)
    dma = pltpu.SemaphoreType.DMA
    scratch = [
        pltpu.VMEM((owners, points), BF16),
        pltpu.VMEM((LANES, points), BF16),
        pltpu.VMEM((rows, LANES), jnp.int32),
        pltpu.VMEM((rows, LANES), jnp.int32),
        pltpu.VMEM((2, size_x + 2, 2, size_y + 2 * PAD, LANES), F32),
        pltpu.VMEM(tile, F32),
        pltpu.VMEM(tile, F32),
        pltpu.VMEM(tile, F32),
        pltpu.VMEM(tile, F32),
        pltpu.VMEM(tile, F32),
        pltpu.VMEM(tile, F32),
        pltpu.VMEM(tile, F32),
        pltpu.VMEM(tile, F32),
        pltpu.VMEM(tile, F32),
        pltpu.VMEM((columns, size_z), F32),
        pltpu.VMEM((size_x, 2 * size_z, size_y), BF16),
        pltpu.VMEM((n_gx, columns, LANES), BF16),
        pltpu.VMEM((n_gx, LANES), jnp.int32),
        pltpu.VMEM((n_gx, LANES), jnp.int32),
        pltpu.VMEM((n_gx, LANES), F32),
        pltpu.VMEM((rows, LANES), F32),
        pltpu.VMEM((2, 2, size_x, 2, 1, LANES), F32),
        pltpu.VMEM((2, 2, size_x, 2, 1, LANES), F32),
        pltpu.VMEM((2, n_gy, 2 * n_gx, LANES), F32),
        pltpu.VMEM((2, n_gy, 2 * n_gx, LANES), F32),
        pltpu.VMEM((2, n_gx, 2, LANES), F32),
        pltpu.VMEM((2, n_gx, 2, LANES), F32),
        pltpu.VMEM((2, n_gx, 2, LANES), F32),
        pltpu.VMEM((2, n_gx, 2, LANES), F32),
        pltpu.VMEM((2, 2 * n_gx, LANES), F32),
        pltpu.VMEM((2, n_gy, 2 * n_gx, LANES), F32),
        pltpu.VMEM((2, LANES), F32),
        pltpu.VMEM((n_gx, 2, LANES), F32),
        pltpu.VMEM((2, LANES), F32),
        pltpu.VMEM((n_gy, 2, LANES), F32),
    ] + [dma((2,))] * 10 + [dma((2, 2))] * 4
    vmem = pl.BlockSpec(memory_space=pltpu.VMEM)
    out = jax.ShapeDtypeStruct((rows, LANES), F32)
    solution, residual = pl.pallas_call(
        functools.partial(kernel, n_gx, n_gy),
        out_shape=(out, out),
        in_specs=[vmem] * 7,
        out_specs=(vmem, vmem),
        scratch_shapes=scratch,
        compiler_params=pltpu.CompilerParams(
            collective_id=0, has_side_effects=True, vmem_limit_bytes=56 * 1024 * 1024
        ),
    )(
        beta,
        jump.reshape(rows, LANES),
        stiff.reshape(rows, LANES),
        weight.reshape(rows, LANES),
        owner.reshape(rows, LANES),
        cell.reshape(rows, LANES),
        count.reshape(1, 1),
    )
    return solution.reshape(points), residual.reshape(points)


def solution(mesh):
    points = P(("gx", "gy"))
    return jax.shard_map(
        functools.partial(on_device, mesh.shape["gx"], mesh.shape["gy"]),
        mesh=mesh,
        in_specs=(P("gx", "gy", None), points, points, points, P(("gx", "gy"), None), points, points),
        out_specs=(points, points),
        check_vma=False,
    )
```

```python
import functools

import jax
import jax.numpy as jnp
from jax import lax
from jax.experimental import pallas as pl
from jax.experimental.pallas import tpu as pltpu
from jax.sharding import PartitionSpec as P

CHEB = 6
SHIFT = 0.01
THETA = 1.025
DELTA = 0.975
SIGMA = THETA / DELTA
EPS = 1e-06
LANES = 128
PAD = 8
MESH = pl.DeviceIdType.MESH
F32 = jnp.float32
BF16 = jnp.bfloat16
CHUNK = 512


def sweep_factors():
    factors = []
    ratio = 1.0 / SIGMA
    for _ in range(CHEB - 1):
        ratio_next = 1.0 / (2.0 * SIGMA - ratio)
        factors.append((ratio_next * ratio, 2.0 * ratio_next / DELTA))
        ratio = ratio_next
    return factors


def least_squares(start, columns):
    count = len(columns)
    targets = [start] + [start * 0.0 for unused in range(count)]
    cosines = []
    sines = []
    upper = []
    for outer in range(count):
        column = list(columns[outer])
        for inner in range(outer):
            first = cosines[inner] * column[inner] + sines[inner] * column[inner + 1]
            second = -sines[inner] * column[inner] + cosines[inner] * column[inner + 1]
            column[inner] = first
            column[inner + 1] = second
        radius = jnp.sqrt(column[outer] * column[outer] + column[outer + 1] * column[outer + 1])
        cosine = column[outer] / radius
        sine = column[outer + 1] / radius
        column[outer] = radius
        targets[outer + 1] = -sine * targets[outer]
        targets[outer] = cosine * targets[outer]
        cosines.append(cosine)
        sines.append(sine)
        upper.append(column)
    coeffs = [None] * count
    for outer in reversed(range(count)):
        total = targets[outer]
        for later in range(outer + 1, count):
            total = total - upper[later][outer] * coeffs[later]
        coeffs[outer] = total / upper[outer][outer]
    return coeffs


def halves(x):
    high = x.astype(BF16)
    low = (x - high.astype(F32)).astype(BF16)
    return high, low


def nt_dot(a, b):
    return lax.dot_general(a, b, (((1,), (1,)), ((), ())), preferred_element_type=F32)


def nn_dot(a, b):
    return lax.dot_general(a, b, (((1,), (0,)), ((), ())), preferred_element_type=F32)


def total(x):
    return jnp.sum(jnp.sum(x, axis=0, keepdims=True), axis=1, keepdims=True)


def pack_row(values):
    lane = lax.broadcasted_iota(jnp.int32, (1, LANES), 1)
    row = jnp.zeros((1, LANES), F32)
    for at, value in enumerate(values):
        row = jnp.where(lane == at, value, row)
    return row


def unpack_row(row, count):
    lane = lax.broadcasted_iota(jnp.int32, (1, LANES), 1)
    return [
        jnp.sum(jnp.where(lane == at, row, 0.0), axis=1, keepdims=True) for at in range(count)
    ]


def kernel(
    n_gx,
    n_gy,
    beta,
    jump,
    stiff,
    weight,
    owner,
    cell,
    count,
    sol,
    res,
    t_one,
    l_one,
    target,
    lanes_at,
    u,
    d,
    g,
    invd,
    axl,
    axh,
    ayl,
    ayh,
    azl,
    azh,
    acc,
    field_t,
    c_one,
    z_at,
    slot_val,
    picked,
    sampled,
    y_send,
    y_recv,
    fa_send,
    fa_recv,
    fb_send,
    fb_recv,
    rb_send,
    rb_recv,
    ra_send,
    ra_recv,
    pb_send,
    pb_recv,
    pa_send,
    pa_recv,
    fa_ss,
    fa_rs,
    fb_ss,
    fb_rs,
    rb_ss,
    rb_rs,
    ra_ss,
    ra_rs,
    p_ss,
    p_rs,
    x_ss,
    x_rs,
    y_ss,
    y_rs,
):
    me_x = lax.axis_index("gx")
    me_y = lax.axis_index("gy")
    size_x, size_y, size_z = beta.shape
    rows = jump.shape[0]
    points = rows * LANES
    owners = n_gx * n_gy
    cap = LANES // n_gy
    slots = n_gx * LANES
    columns = size_x * size_y
    chunk = min(CHUNK, slots)
    lane8 = lax.broadcasted_iota(jnp.int32, (PAD, LANES), 1)

    def at_gx(shift):
        return {"gx": lax.rem(me_x + shift + n_gx, n_gx), "gy": me_y}

    def at_gy(shift):
        return {"gx": me_x, "gy": lax.rem(me_y + shift + n_gy, n_gy)}

    for p in range(2):
        for x in (0, size_x + 1):
            u[p, x] = jnp.zeros(u.shape[2:], F32)
    zero_tile = jnp.zeros((2, PAD, LANES), F32)

    def clear(x, _):
        for p in range(2):
            u[p, x, :, 0:PAD, :] = zero_tile
            u[p, x, :, PAD + size_y : 2 * PAD + size_y, :] = zero_tile
        return 0

    lax.fori_loop(1, size_x + 1, clear, 0)

    barrier = pltpu.get_barrier_semaphore()

    def greet_x(k, _):
        pl.semaphore_signal(barrier, inc=1, device_id=at_gx(k), device_id_type=MESH)
        return 0

    def greet_y(k, _):
        pl.semaphore_signal(barrier, inc=1, device_id=at_gy(k), device_id_type=MESH)
        return 0

    lax.fori_loop(1, n_gx, greet_x, 0)
    lax.fori_loop(1, n_gy, greet_y, 0)

    def gx_copy(src, dst, send, recv, k, sign):
        return pltpu.make_async_remote_copy(
            src_ref=src,
            dst_ref=dst,
            send_sem=send,
            recv_sem=recv,
            device_id=at_gx(sign * k),
            device_id_type=MESH,
        )

    def gy_copy(src, dst, send, recv, k, sign):
        return pltpu.make_async_remote_copy(
            src_ref=src,
            dst_ref=dst,
            send_sem=send,
            recv_sem=recv,
            device_id=at_gy(sign * k),
            device_id_type=MESH,
        )

    def wait_for(ref, sem):
        pltpu.make_async_copy(ref, ref, sem).wait()

    def send_gx(src, dst, send, recv, sign):
        def body(k, _):
            gx_copy(src.at[k], dst.at[k], send, recv, k, sign).start()
            return 0

        lax.fori_loop(1, n_gx, body, 0)

    def halo_copies(p, which):
        rows_in = pl.ds(PAD, size_y)
        copies = (
            (
                me_x > 0,
                lambda: gx_copy(
                    u.at[p, 1, :, rows_in, :],
                    u.at[p, size_x + 1, :, rows_in, :],
                    x_ss.at[p, 0],
                    x_rs.at[p, 1],
                    1,
                    -1,
                ),
            ),
            (
                me_x < n_gx - 1,
                lambda: gx_copy(
                    u.at[p, size_x, :, rows_in, :],
                    u.at[p, 0, :, rows_in, :],
                    x_ss.at[p, 1],
                    x_rs.at[p, 0],
                    1,
                    1,
                ),
            ),
            (
                me_y > 0,
                lambda: gy_copy(
                    y_send.at[p, 0], y_recv.at[p, 1], y_ss.at[p, 0], y_rs.at[p, 1], 1, -1
                ),
            ),
            (
                me_y < n_gy - 1,
                lambda: gy_copy(
                    y_send.at[p, 1], y_recv.at[p, 0], y_ss.at[p, 1], y_rs.at[p, 0], 1, 1
                ),
            ),
        )
        return [copies[i] for i in which]

    def halo_send_x(p):
        for on, copy in halo_copies(p, (0, 1)):
            pl.when(on)(lambda: copy().start())

    def halo_send_y(p):
        def pack(x, _):
            for h in range(2):
                y_send[p, 0, x, h] = u[p, x + 1, h, PAD : PAD + 1, :]
                y_send[p, 1, x, h] = u[p, x + 1, h, PAD + size_y - 1 : PAD + size_y, :]
            return 0

        lax.fori_loop(0, size_x, pack, 0)
        for on, copy in halo_copies(p, (2, 3)):
            pl.when(on)(lambda: copy().start())

    def halo_wait_sent(p):
        for on, copy in halo_copies(p, range(4)):
            pl.when(on)(lambda: copy().wait_send())

    def halo_wait(p):
        (_, down_x), (_, up_x), (_, down_y), (_, up_y) = halo_copies(p, range(4))
        pl.when(me_x < n_gx - 1)(lambda: down_x().wait_recv())
        pl.when(me_x > 0)(lambda: up_x().wait_recv())

        @pl.when(me_y < n_gy - 1)
        def _():
            down_y().wait_recv()

            def unpack(x, _):
                for h in range(2):
                    u[p, x + 1, h, PAD + size_y : PAD + size_y + 1, :] = y_recv[p, 1, x, h]
                return 0

            lax.fori_loop(0, size_x, unpack, 0)

        @pl.when(me_y > 0)
        def _():
            up_y().wait_recv()

            def unpack(x, _):
                for h in range(2):
                    u[p, x + 1, h, PAD - 1 : PAD, :] = y_recv[p, 0, x, h]
                return 0

            lax.fori_loop(0, size_x, unpack, 0)

    shift_gy = n_gy.bit_length() - 1
    own = owner[...]
    target[...] = ((own & (n_gy - 1)) - me_y & (n_gy - 1)) * n_gx + (
        (own >> shift_gy) - me_x & (n_gx - 1)
    )
    iota_t = lax.broadcasted_iota(jnp.int32, (owners, LANES), 0)
    iota_l = lax.broadcasted_iota(jnp.int32, (LANES, LANES), 0)
    above = lax.broadcasted_iota(jnp.int32, (LANES, 2 * LANES), 1)
    below = lax.broadcasted_iota(jnp.int32, (LANES, 2 * LANES), 0)
    counter = ((below < above) | (above >= LANES)).astype(BF16)
    offset = jnp.zeros((owners, LANES), F32)
    for j in range(rows):
        hit = target[j : j + 1, :] == iota_t
        hit_f = jnp.where(hit, 1.0, 0.0)
        hit_b = hit_f.astype(BF16)
        t_one[:, j * LANES : (j + 1) * LANES] = hit_b
        both = nn_dot(hit_b, counter)
        rank = jnp.sum(hit_f * (both[:, :LANES] + offset), axis=0, keepdims=True)
        offset = offset + both[:, LANES:]
        lane_of = rank.astype(jnp.int32) + me_y * cap
        l_one[:, j * LANES : (j + 1) * LANES] = jnp.where(lane_of == iota_l, 1.0, 0.0).astype(BF16)

    def to_rows(vector, row_of):
        out = jnp.zeros((owners, LANES), F32)
        for j in range(rows):
            cols = slice(j * LANES, (j + 1) * LANES)
            for part in row_of(vector[j : j + 1, :]):
                spread = t_one[:, cols] * part
                out = out + nt_dot(spread, l_one[:, cols])
        return out

    def split_index(row):
        low = (row & (2 * LANES - 1)) + 1
        middle = (row >> 8) & (2 * LANES - 1)
        high = row >> 16
        return [
            x.astype(F32).astype(BF16) for x in (low, middle * 256, high * 65536)
        ]

    def forward_a(f, first, second):
        for k in range(n_gy):
            fa_send[f, k, 0:n_gx, :] = first[k * n_gx : (k + 1) * n_gx, :]
            fa_send[f, k, n_gx : 2 * n_gx, :] = second[k]
        for k in range(1, n_gy):
            gy_copy(fa_send.at[f, k], fa_recv.at[f, k], fa_ss.at[f], fa_rs.at[f], k, 1).start()

    def forward_b(f):
        wait_for(fa_recv.at[f, pl.ds(1, n_gy - 1)], fa_rs.at[f])
        both = fa_send[f, 0]
        for k in range(1, n_gy):
            both = both + fa_recv[f, k]
        for k in range(n_gx):
            fb_send[f, k, 0:1, :] = both[k : k + 1, :]
            fb_send[f, k, 1:2, :] = both[n_gx + k : n_gx + k + 1, :]
        send_gx(fb_send.at[f], fb_recv.at[f], fb_ss.at[f], fb_rs.at[f], 1)
        fb_recv[f, 0] = fb_send[f, 0]

    def forward_c(f):
        wait_for(fb_recv.at[f, pl.ds(1, n_gx - 1)], fb_rs.at[f])
        return fb_recv[f, :, 0, :], fb_recv[f, :, 1, :]

    def back_a(f, second):
        for k in range(n_gx):
            rb_send[f, k, 0:1, :] = picked[k : k + 1, :]
            rb_send[f, k, 1:2, :] = second
        send_gx(rb_send.at[f], rb_recv.at[f], rb_ss.at[f], rb_rs.at[f], -1)
        rb_recv[f, 0] = rb_send[f, 0]

    def back_b(f):
        wait_for(rb_recv.at[f, pl.ds(1, n_gx - 1)], rb_rs.at[f])
        ra_send[f, 0:n_gx, :] = rb_recv[f, :, 0, :]
        ra_send[f, n_gx : 2 * n_gx, :] = rb_recv[f, :, 1, :]
        for k in range(1, n_gy):
            gy_copy(ra_send.at[f], ra_recv.at[f, k], ra_ss.at[f], ra_rs.at[f], k, -1).start()

    def back_c(f):
        wait_for(ra_recv.at[f, pl.ds(1, n_gy - 1)], ra_rs.at[f])
        blocks = [ra_send[f]] + [ra_recv[f, k] for k in range(1, n_gy)]
        high, low = halves(jnp.concatenate([b[0:n_gx, :] for b in blocks], axis=0))
        rest = blocks[0][n_gx:, :]
        for b in blocks[1:]:
            rest = rest + b[n_gx:, :]
        for j in range(rows):
            cols = slice(j * LANES, (j + 1) * LANES)
            lanes = l_one[:, cols]
            found = nn_dot(high, lanes) + nn_dot(low, lanes)
            sampled[j : j + 1, :] = jnp.sum(
                found * t_one[:, cols].astype(F32), axis=0, keepdims=True
            )
        return sampled[...], jnp.sum(rest, axis=0, keepdims=True)

    live = lax.broadcasted_iota(jnp.int32, (rows, LANES), 0) < count[...]
    rhs = jnp.where(live, jump[...], 0.0)
    sw = weight[...]
    cells = cell[...]
    index_rows = to_rows(cells, split_index)
    value_rows = to_rows(sw * rhs, halves)
    pl.semaphore_wait(barrier, n_gx + n_gy - 2)
    forward_a(0, index_rows, [value_rows[k * n_gx : (k + 1) * n_gx, :] for k in range(n_gy)])

    def place(x, _):
        for h in range(2):
            u[1, x + 1, h, PAD : PAD + size_y, :] = beta[x, :, h * LANES : (h + 1) * LANES]
        return 0

    lax.fori_loop(0, size_x, place, 0)
    halo_send_x(1)
    halo_send_y(1)
    forward_b(0)

    def rows_at(ref, p, x, h, start, n):
        return ref[p, x, h, pl.ds(start, n), :]

    def z_sides(low, high, lane):
        low_up, high_up = pltpu.roll(low, 1, 1), pltpu.roll(high, 1, 1)
        low_dn, high_dn = pltpu.roll(low, LANES - 1, 1), pltpu.roll(high, LANES - 1, 1)
        return (
            (low_up, jnp.where(lane == 0, low_up, high_up)),
            (jnp.where(lane == LANES - 1, high_dn, low_dn), high_dn),
        )

    def harmonic(a, b):
        return 2.0 * a * b / (a + b)

    halo_wait(1)

    def coefficients(x, y):
        centre = [rows_at(u, 1, x + 1, h, y + PAD, PAD) for h in range(2)]
        before, after = z_sides(centre[0], centre[1], lane8)
        for h in range(2):
            c = centre[h]
            kxl = harmonic(c, rows_at(u, 1, x, h, y + PAD, PAD))
            kxh = harmonic(c, rows_at(u, 1, x + 2, h, y + PAD, PAD))
            kyl = harmonic(c, rows_at(u, 1, x + 1, h, y + PAD - 1, PAD))
            kyh = harmonic(c, rows_at(u, 1, x + 1, h, y + PAD + 1, PAD))
            kzl = harmonic(c, before[h])
            kzh = harmonic(c, after[h])
            if h == 0:
                kzl = jnp.where(lane8 == 0, 0.0, kzl)
            else:
                kzh = jnp.where(lane8 == LANES - 1, 0.0, kzh)
            inverse = 1.0 / (SHIFT + kxl + kxh + kyl + kyh + kzl + kzh)
            at = (x, h, pl.ds(y, PAD), slice(None))
            invd[at] = inverse
            axl[at] = kxl * inverse
            axh[at] = kxh * inverse
            ayl[at] = kyl * inverse
            ayh[at] = kyh * inverse
            azl[at] = kzl * inverse
            azh[at] = kzh * inverse

    def coefficient_planes(i, _):
        for x in range(2):
            for y in range(0, size_y, PAD):
                coefficients(2 * i + x, y)
        return 0

    lax.fori_loop(0, size_x // 2, coefficient_planes, 0)
    halo_wait_sent(1)

    index, values = forward_c(0)
    index = index.astype(jnp.int32) - 1
    z_at[...] = jnp.where(index < 0, -1, index & (size_z - 1))
    slot_val[...] = index >> 8
    iota_c = lax.broadcasted_iota(jnp.int32, (columns, LANES), 0)
    per = chunk // LANES

    def column_table(j, _):
        row = slot_val[pl.ds(j, 1), :]
        c_one[j] = jnp.where(row == iota_c, 1.0, 0.0).astype(BF16)
        return 0

    lax.fori_loop(0, n_gx, column_table, 0)
    iota_z = lax.broadcasted_iota(jnp.int32, (size_z, LANES), 0)

    def spread_grid(values):
        picked[...] = values
        acc[...] = jnp.zeros_like(acc)

        def body(i, _):
            high_parts, low_parts, col_parts = [], [], []
            for q in range(per):
                j = i * per + q
                row = picked[pl.ds(j, 1), :]
                hit = z_at[pl.ds(j, 1), :] == iota_z
                high = row.astype(BF16).astype(F32)
                high_parts.append(jnp.where(hit, high, 0.0).astype(BF16))
                low_parts.append(jnp.where(hit, row - high, 0.0).astype(BF16))
                col_parts.append(c_one[j])
            cols = jnp.concatenate(col_parts, axis=1)
            acc[...] += nt_dot(cols, jnp.concatenate(high_parts, axis=1)) + nt_dot(
                cols, jnp.concatenate(low_parts, axis=1)
            )
            return 0

        lax.fori_loop(0, slots // chunk, body, 0)

    def sample_grid(p):
        def turn(x, _):
            for h in range(2):
                high, low = halves(u[p, x + 1, h, PAD : PAD + size_y, :].T)
                field_t[x, h * LANES : (h + 1) * LANES, :] = high
                field_t[x, size_z + h * LANES : size_z + (h + 1) * LANES, :] = low
            return 0

        lax.fori_loop(0, size_x, turn, 0)
        whole = jnp.concatenate([field_t[x] for x in range(size_x)], axis=1)

        def body(i, _):
            found = nn_dot(
                whole, jnp.concatenate([c_one[i * per + q] for q in range(per)], axis=1)
            )
            for q in range(per):
                j = i * per + q
                hit = z_at[pl.ds(j, 1), :] == iota_z
                cols = slice(q * LANES, (q + 1) * LANES)
                both = found[:size_z, cols] + found[size_z:, cols]
                picked[pl.ds(j, 1), :] = jnp.sum(
                    jnp.where(hit, both, 0.0), axis=0, keepdims=True
                )
            return 0

        lax.fori_loop(0, slots // chunk, body, 0)

    def relax(p, x, y, n, first, second):
        lane = lax.broadcasted_iota(jnp.int32, (n, LANES), 1)
        centre = [rows_at(u, p, x + 1, h, y + PAD, n) for h in range(2)]
        before, after = z_sides(centre[0], centre[1], lane)
        for h in range(2):
            at = (x, h, pl.ds(y, n), slice(None))
            image = g[at] - centre[h]
            image += axl[at] * rows_at(u, p, x, h, y + PAD, n)
            image += axh[at] * rows_at(u, p, x + 2, h, y + PAD, n)
            image += ayl[at] * rows_at(u, p, x + 1, h, y + PAD - 1, n)
            image += ayh[at] * rows_at(u, p, x + 1, h, y + PAD + 1, n)
            image += azl[at] * before[h] + azh[at] * after[h]
            update = first * d[at] + second * image
            d[at] = update
            u[1 - p, x + 1, h, pl.ds(y + PAD, n), :] = centre[h] + update

    def pressure():
        def begin(x, _):
            for h in range(2):
                source = acc[pl.ds(x * size_y, size_y), h * LANES : (h + 1) * LANES]
                scaled = source * invd[x, h]
                g[x, h] = scaled
                scaled = scaled * (1.0 / THETA)
                d[x, h] = scaled
                u[0, x + 1, h, PAD : PAD + size_y, :] = scaled
            return 0

        lax.fori_loop(0, size_x, begin, 0)
        halo_send_x(0)
        halo_send_y(0)
        for step, (first, second) in enumerate(sweep_factors()):
            p = step % 2
            last = step == CHEB - 2
            halo_wait(p)
            if step > 0:
                halo_wait_sent(1 - p)

            for x in (0, size_x - 1):
                for y in range(0, size_y, 2 * PAD):
                    relax(p, x, y, 2 * PAD, first, second)
            if not last:
                halo_send_x(1 - p)
            middle = range(1, size_x - 1)
            for x in middle:
                relax(p, x, 0, PAD, first, second)
                relax(p, x, size_y - PAD, PAD, first, second)
            if not last:
                halo_send_y(1 - p)
            for x in middle:
                for y in range(PAD, size_y - PAD, 2 * PAD):
                    relax(p, x, y, 2 * PAD, first, second)
        halo_wait_sent((CHEB - 2) % 2)
        return (CHEB - 1) % 2

    zero_row = jnp.zeros((1, LANES), F32)
    spread_grid(values)
    sample_grid(pressure())
    back_a(0, zero_row)
    back_b(0)
    got, _ = back_c(0)
    steady = stiff[...]
    image_1 = jnp.where(live, steady * rhs + sw * got, 0.0)

    partial = pack_row([total(rhs * rhs), total(rhs * image_1), total(image_1 * image_1)])
    partial_rows = jnp.broadcast_to(partial, (n_gx, LANES))
    forward_a(1, to_rows(sw * image_1, halves), [partial_rows] * n_gy)
    forward_b(1)
    values, sums = forward_c(1)
    sum_bb, sum_ab, _ = unpack_row(jnp.sum(sums, axis=0, keepdims=True), 3)
    start = jnp.sqrt(sum_bb + EPS)
    scale = 1.0 / start
    v_1 = rhs * scale
    w_1 = image_1 * scale
    h_11 = sum_ab * scale * scale
    rest_1 = w_1 - h_11 * v_1
    spread_grid(values)
    sample_grid(pressure())
    back_a(1, pack_row([total(rest_1 * rest_1)]))
    back_b(1)
    got, sums = back_c(1)
    image_2 = jnp.where(live, steady * image_1 + sw * got, 0.0)
    h_21 = jnp.sqrt(unpack_row(sums, 1)[0] + EPS)
    v_2 = rest_1 / h_21
    w_2 = (image_2 * scale - h_11 * w_1) / h_21

    partial = pack_row(
        [total(w_2 * v_1), total(w_2 * v_2), total(w_2 * w_2), total(v_1 * v_1), total(v_1 * v_2),
         total(v_2 * v_2)]
    )
    pb_send[...] = jnp.broadcast_to(partial, pb_send.shape)

    def spill(k, _):
        gx_copy(pb_send, pb_recv.at[k], p_ss.at[0], p_rs.at[0], k, 1).start()
        return 0

    lax.fori_loop(1, n_gx, spill, 0)
    pb_recv[0] = pb_send[...]
    wait_for(pb_recv.at[pl.ds(1, n_gx - 1)], p_rs.at[0])
    pa_send[...] = jnp.sum(pb_recv[...], axis=0)
    for k in range(1, n_gy):
        gy_copy(pa_send, pa_recv.at[k], p_ss.at[1], p_rs.at[1], k, 1).start()
    pa_recv[0] = pa_send[...]
    wait_for(pa_recv.at[pl.ds(1, n_gy - 1)], p_rs.at[1])
    sums = jnp.sum(pa_recv[...], axis=0)[0:1, :]
    w2v1, w2v2, w2w2, v1v1, v1v2, v2v2 = unpack_row(sums, 6)
    h_12 = w2v1
    h_22 = w2v2 - h_12 * v1v2
    square = (
        w2w2
        + h_12 * h_12 * v1v1
        + h_22 * h_22 * v2v2
        - 2.0 * h_12 * w2v1
        - 2.0 * h_22 * w2v2
        + 2.0 * h_12 * h_22 * v1v2
    )
    h_32 = jnp.sqrt(jnp.maximum(square, 0.0) + EPS)
    y_1, y_2 = least_squares(start, [[h_11, h_21], [h_12, h_22, h_32]])
    sol[...] = y_1 * v_1 + y_2 * v_2
    res[...] = rhs - y_1 * w_1 - y_2 * w_2

    for f in range(2):
        for k in range(1, n_gy):
            gy_copy(fa_send.at[f, k], fa_recv.at[f, k], fa_ss.at[f], fa_rs.at[f], k, 1).wait_send()
            gy_copy(ra_send.at[f], ra_recv.at[f, k], ra_ss.at[f], ra_rs.at[f], k, -1).wait_send()
        wait_for(fb_send.at[f, pl.ds(1, n_gx - 1)], fb_ss.at[f])
        wait_for(rb_send.at[f, pl.ds(1, n_gx - 1)], rb_ss.at[f])
    wait_for(pb_recv.at[pl.ds(1, n_gx - 1)], p_ss.at[0])
    wait_for(pa_recv.at[pl.ds(1, n_gy - 1)], p_ss.at[1])


def on_device(n_gx, n_gy, beta, jump, stiff, weight, owner, cell, count):
    size_x, size_y, size_z = beta.shape
    points = jump.shape[0]
    rows = points // LANES
    owners = n_gx * n_gy
    columns = size_x * size_y
    tile = (size_x, 2, size_y, LANES)
    dma = pltpu.SemaphoreType.DMA
    scratch = [
        pltpu.VMEM((owners, points), BF16),
        pltpu.VMEM((LANES, points), BF16),
        pltpu.VMEM((rows, LANES), jnp.int32),
        pltpu.VMEM((rows, LANES), jnp.int32),
        pltpu.VMEM((2, size_x + 2, 2, size_y + 2 * PAD, LANES), F32),
        pltpu.VMEM(tile, F32),
        pltpu.VMEM(tile, F32),
        pltpu.VMEM(tile, F32),
        pltpu.VMEM(tile, F32),
        pltpu.VMEM(tile, F32),
        pltpu.VMEM(tile, F32),
        pltpu.VMEM(tile, F32),
        pltpu.VMEM(tile, F32),
        pltpu.VMEM(tile, F32),
        pltpu.VMEM((columns, size_z), F32),
        pltpu.VMEM((size_x, 2 * size_z, size_y), BF16),
        pltpu.VMEM((n_gx, columns, LANES), BF16),
        pltpu.VMEM((n_gx, LANES), jnp.int32),
        pltpu.VMEM((n_gx, LANES), jnp.int32),
        pltpu.VMEM((n_gx, LANES), F32),
        pltpu.VMEM((rows, LANES), F32),
        pltpu.VMEM((2, 2, size_x, 2, 1, LANES), F32),
        pltpu.VMEM((2, 2, size_x, 2, 1, LANES), F32),
        pltpu.VMEM((2, n_gy, 2 * n_gx, LANES), F32),
        pltpu.VMEM((2, n_gy, 2 * n_gx, LANES), F32),
        pltpu.VMEM((2, n_gx, 2, LANES), F32),
        pltpu.VMEM((2, n_gx, 2, LANES), F32),
        pltpu.VMEM((2, n_gx, 2, LANES), F32),
        pltpu.VMEM((2, n_gx, 2, LANES), F32),
        pltpu.VMEM((2, 2 * n_gx, LANES), F32),
        pltpu.VMEM((2, n_gy, 2 * n_gx, LANES), F32),
        pltpu.VMEM((2, LANES), F32),
        pltpu.VMEM((n_gx, 2, LANES), F32),
        pltpu.VMEM((2, LANES), F32),
        pltpu.VMEM((n_gy, 2, LANES), F32),
    ] + [dma((2,))] * 10 + [dma((2, 2))] * 4
    vmem = pl.BlockSpec(memory_space=pltpu.VMEM)
    out = jax.ShapeDtypeStruct((rows, LANES), F32)
    solution, residual = pl.pallas_call(
        functools.partial(kernel, n_gx, n_gy),
        out_shape=(out, out),
        in_specs=[vmem] * 7,
        out_specs=(vmem, vmem),
        scratch_shapes=scratch,
        compiler_params=pltpu.CompilerParams(
            collective_id=0, has_side_effects=True, vmem_limit_bytes=56 * 1024 * 1024
        ),
    )(
        beta,
        jump.reshape(rows, LANES),
        stiff.reshape(rows, LANES),
        weight.reshape(rows, LANES),
        owner.reshape(rows, LANES),
        cell.reshape(rows, LANES),
        count.reshape(1, 1),
    )
    return solution.reshape(points), residual.reshape(points)


def solution(mesh):
    points = P(("gx", "gy"))
    return jax.shard_map(
        functools.partial(on_device, mesh.shape["gx"], mesh.shape["gy"]),
        mesh=mesh,
        in_specs=(P("gx", "gy", None), points, points, points, P(("gx", "gy"), None), points, points),
        out_specs=(points, points),
        check_vma=False,
    )
```

```python
import functools

import jax
import jax.numpy as jnp
from jax import lax
from jax.experimental import pallas as pl
from jax.experimental.pallas import tpu as pltpu
from jax.sharding import PartitionSpec as P

CHEB = 6
SHIFT = 0.01
THETA = 1.025
DELTA = 0.975
SIGMA = THETA / DELTA
EPS = 1e-06
LANES = 128
PAD = 8
EDGE = 2 * PAD
PARTS = 2
DEPTH = CHEB - 1
SIDES = [(x, y) for x in (-1, 0, 1) for y in (-1, 0, 1) if (x, y) != (0, 0)]
MESH = pl.DeviceIdType.MESH
F32 = jnp.float32
BF16 = jnp.bfloat16
CHUNK = 512


def sweep_factors():
    factors = []
    ratio = 1.0 / SIGMA
    for _ in range(CHEB - 1):
        ratio_next = 1.0 / (2.0 * SIGMA - ratio)
        factors.append((ratio_next * ratio, 2.0 * ratio_next / DELTA))
        ratio = ratio_next
    return factors


def least_squares(start, columns):
    count = len(columns)
    targets = [start] + [start * 0.0 for unused in range(count)]
    cosines = []
    sines = []
    upper = []
    for outer in range(count):
        column = list(columns[outer])
        for inner in range(outer):
            first = cosines[inner] * column[inner] + sines[inner] * column[inner + 1]
            second = -sines[inner] * column[inner] + cosines[inner] * column[inner + 1]
            column[inner] = first
            column[inner + 1] = second
        radius = jnp.sqrt(column[outer] * column[outer] + column[outer + 1] * column[outer + 1])
        cosine = column[outer] / radius
        sine = column[outer + 1] / radius
        column[outer] = radius
        targets[outer + 1] = -sine * targets[outer]
        targets[outer] = cosine * targets[outer]
        cosines.append(cosine)
        sines.append(sine)
        upper.append(column)
    coeffs = [None] * count
    for outer in reversed(range(count)):
        total = targets[outer]
        for later in range(outer + 1, count):
            total = total - upper[later][outer] * coeffs[later]
        coeffs[outer] = total / upper[outer][outer]
    return coeffs


def halves(x):
    high = x.astype(BF16)
    low = (x - high.astype(F32)).astype(BF16)
    return high, low


def nt_dot(a, b):
    return lax.dot_general(a, b, (((1,), (1,)), ((), ())), preferred_element_type=F32)


def nn_dot(a, b):
    return lax.dot_general(a, b, (((1,), (0,)), ((), ())), preferred_element_type=F32)


def total(x):
    return jnp.sum(jnp.sum(x, axis=0, keepdims=True), axis=1, keepdims=True)


def pack_row(values):
    lane = lax.broadcasted_iota(jnp.int32, (1, LANES), 1)
    row = jnp.zeros((1, LANES), F32)
    for at, value in enumerate(values):
        row = jnp.where(lane == at, value, row)
    return row


def unpack_row(row, count):
    lane = lax.broadcasted_iota(jnp.int32, (1, LANES), 1)
    return [
        jnp.sum(jnp.where(lane == at, row, 0.0), axis=1, keepdims=True) for at in range(count)
    ]


def kernel(
    n_gx,
    n_gy,
    beta,
    jump,
    stiff,
    weight,
    owner,
    cell,
    count,
    sol,
    res,
    t_one,
    l_one,
    target,
    lanes_at,
    rim,
    u,
    d,
    invd,
    axl,
    axh,
    ayl,
    ayh,
    azl,
    azh,
    field_t,
    c_one,
    z_high,
    z_low,
    z_at,
    slot_val,
    picked,
    sampled,
    fa_send,
    fa_recv,
    fb_send,
    fb_recv,
    rb_send,
    rb_recv,
    ra_send,
    ra_recv,
    pb_send,
    pb_recv,
    pa_send,
    pa_recv,
    a_ss,
    a_rs,
    b_ss,
    b_rs,
    p_ss,
    p_rs,
    rim_ss,
    rim_rs,
):
    me_x = lax.axis_index("gx")
    me_y = lax.axis_index("gy")
    size_x, size_y, size_z = beta.shape
    rows = jump.shape[0]
    points = rows * LANES
    owners = n_gx * n_gy
    cap = LANES // n_gy
    slots = n_gx * LANES
    columns = size_x * size_y
    chunk = min(CHUNK, slots)
    lane8 = lax.broadcasted_iota(jnp.int32, (PAD, LANES), 1)

    def at_gx(shift):
        return {"gx": lax.rem(me_x + shift + n_gx, n_gx), "gy": me_y}

    def at_gy(shift):
        return {"gx": me_x, "gy": lax.rem(me_y + shift + n_gy, n_gy)}

    def clear(x, _):
        rim[x] = jnp.zeros(rim.shape[1:], F32)
        return 0

    lax.fori_loop(0, rim.shape[0], clear, 0)

    barrier = pltpu.get_barrier_semaphore()

    def greet_x(k, _):
        pl.semaphore_signal(barrier, inc=1, device_id=at_gx(k), device_id_type=MESH)
        return 0

    def greet_y(k, _):
        pl.semaphore_signal(barrier, inc=1, device_id=at_gy(k), device_id_type=MESH)
        return 0

    lax.fori_loop(1, n_gx, greet_x, 0)
    lax.fori_loop(1, n_gy, greet_y, 0)
    for side_x, side_y in SIDES:
        if side_x * side_y:
            corner = {"gx": at_gx(side_x)["gx"], "gy": at_gy(side_y)["gy"]}
            pl.semaphore_signal(barrier, inc=1, device_id=corner, device_id_type=MESH)

    def gx_copy(src, dst, send, recv, k, sign):
        return pltpu.make_async_remote_copy(
            src_ref=src,
            dst_ref=dst,
            send_sem=send,
            recv_sem=recv,
            device_id=at_gx(sign * k),
            device_id_type=MESH,
        )

    def gy_copy(src, dst, send, recv, k, sign):
        return pltpu.make_async_remote_copy(
            src_ref=src,
            dst_ref=dst,
            send_sem=send,
            recv_sem=recv,
            device_id=at_gy(sign * k),
            device_id_type=MESH,
        )

    def wait_for(ref, sem):
        pltpu.make_async_copy(ref, ref, sem).wait()

    def send_gx(src, dst, send, recv, sign):
        def body(k, _):
            gx_copy(src.at[k], dst.at[k], send, recv, k, sign).start()
            return 0

        lax.fori_loop(1, n_gx, body, 0)

    planes = size_x + 2 * DEPTH

    def inside(x, y):
        return (x >= 0) & (x < n_gx) & (y >= 0) & (y < n_gy)

    def rim_copies(f):
        span_x = {
            -1: (DEPTH, DEPTH + size_x, DEPTH),
            0: (DEPTH, DEPTH, size_x),
            1: (size_x, 0, DEPTH),
        }
        span_y = {
            -1: (EDGE, EDGE + size_y, PAD),
            0: (EDGE, EDGE, size_y),
            1: (EDGE + size_y - PAD, EDGE - PAD, PAD),
        }
        for i, (side_x, side_y) in enumerate(SIDES):
            def copy(i=i, side_x=side_x, side_y=side_y, x=span_x[side_x], y=span_y[side_y]):
                return pltpu.make_async_remote_copy(
                    src_ref=rim_part(f, x[0], x[2], y[0], y[2]),
                    dst_ref=rim_part(f, x[1], x[2], y[1], y[2]),
                    send_sem=rim_ss.at[f, i],
                    recv_sem=rim_rs.at[f, i],
                    device_id={"gx": at_gx(side_x)["gx"], "gy": at_gy(side_y)["gy"]},
                    device_id_type=MESH,
                )

            yield (
                inside(me_x + side_x, me_y + side_y),
                inside(me_x - side_x, me_y - side_y),
                copy,
            )

    def rim_part(f, x, count_x, y, count_y):
        return rim.at[pl.ds(f * planes + x, count_x), :, pl.ds(y, count_y), :]

    def rim_send(f):
        for sent, _, copy in rim_copies(f):
            pl.when(sent)(lambda: copy().start())

    def rim_wait(f):
        for _, received, copy in rim_copies(f):
            pl.when(received)(lambda: copy().wait_recv())

    def rim_wait_sent(f):
        for sent, _, copy in rim_copies(f):
            pl.when(sent)(lambda: copy().wait_send())

    shift_gy = n_gy.bit_length() - 1
    own = owner[...]
    target[...] = ((own & (n_gy - 1)) - me_y & (n_gy - 1)) * n_gx + (
        (own >> shift_gy) - me_x & (n_gx - 1)
    )
    iota_t = lax.broadcasted_iota(jnp.int32, (owners, LANES), 0)
    iota_l = lax.broadcasted_iota(jnp.int32, (LANES, LANES), 0)
    above = lax.broadcasted_iota(jnp.int32, (LANES, 2 * LANES), 1)
    below = lax.broadcasted_iota(jnp.int32, (LANES, 2 * LANES), 0)
    counter = ((below < above) | (above >= LANES)).astype(BF16)
    offset = jnp.zeros((owners, LANES), F32)
    for j in range(rows):
        hit = target[j : j + 1, :] == iota_t
        hit_f = jnp.where(hit, 1.0, 0.0)
        hit_b = hit_f.astype(BF16)
        t_one[:, j * LANES : (j + 1) * LANES] = hit_b
        both = nn_dot(hit_b, counter)
        rank = jnp.sum(hit_f * (both[:, :LANES] + offset), axis=0, keepdims=True)
        offset = offset + both[:, LANES:]
        lane_of = rank.astype(jnp.int32) + me_y * cap
        l_one[:, j * LANES : (j + 1) * LANES] = jnp.where(lane_of == iota_l, 1.0, 0.0).astype(BF16)

    def to_rows(vector, row_of):
        out = jnp.zeros((owners, LANES), F32)
        for j in range(rows):
            cols = slice(j * LANES, (j + 1) * LANES)
            for part in row_of(vector[j : j + 1, :]):
                spread = t_one[:, cols] * part
                out = out + nt_dot(spread, l_one[:, cols])
        return out

    def split_index(row):
        low = (row & (2 * LANES - 1)) + 1
        middle = (row >> 8) & (2 * LANES - 1)
        high = row >> 16
        return [
            x.astype(F32).astype(BF16) for x in (low, middle * 256, high * 65536)
        ]

    def forward_a(fields):
        for k in range(n_gy):
            for i, field in enumerate(fields):
                fa_send[k, i * n_gx : (i + 1) * n_gx, :] = field[k * n_gx : (k + 1) * n_gx, :]
        for k in range(1, n_gy):
            gy_copy(fa_send.at[k], fa_recv.at[k], a_ss.at[0], a_rs.at[0], k, 1).start()

    def forward_b():
        wait_for(fa_recv.at[pl.ds(1, n_gy - 1)], a_rs.at[0])
        both = fa_send[0]
        for k in range(1, n_gy):
            both = both + fa_recv[k]
        for k in range(n_gx):
            for i in range(4):
                fb_send[k, i : i + 1, :] = both[i * n_gx + k : i * n_gx + k + 1, :]
        send_gx(fb_send, fb_recv, b_ss.at[0], b_rs.at[0], 1)
        fb_recv[0] = fb_send[0]

    def forward_c():
        wait_for(fb_recv.at[pl.ds(1, n_gx - 1)], b_rs.at[0])
        return [fb_recv[:, i, :] for i in range(4)]

    def back_a(first, second, sums):
        for k in range(n_gx):
            rb_send[k, 0:1, :] = first[k : k + 1, :]
            rb_send[k, 1:2, :] = second[k : k + 1, :]
            rb_send[k, 2:3, :] = sums
            rb_send[k, 3:4, :] = sums
        send_gx(rb_send, rb_recv, b_ss.at[1], b_rs.at[1], -1)
        rb_recv[0] = rb_send[0]

    def back_b():
        wait_for(rb_recv.at[pl.ds(1, n_gx - 1)], b_rs.at[1])
        ra_send[0:n_gx, :] = rb_recv[:, 0, :]
        ra_send[n_gx : 2 * n_gx, :] = rb_recv[:, 1, :]
        sums = jnp.sum(rb_recv[:, 2, :], axis=0, keepdims=True)
        ra_send[2 * n_gx : 2 * n_gx + PAD, :] = jnp.broadcast_to(sums, (PAD, LANES))
        for k in range(1, n_gy):
            gy_copy(ra_send, ra_recv.at[k], a_ss.at[1], a_rs.at[1], k, -1).start()

    def back_c():
        wait_for(ra_recv.at[pl.ds(1, n_gy - 1)], a_rs.at[1])
        blocks = [ra_send[...]] + [ra_recv[k] for k in range(1, n_gy)]
        sums = blocks[0][2 * n_gx : 2 * n_gx + 1, :]
        for b in blocks[1:]:
            sums = sums + b[2 * n_gx : 2 * n_gx + 1, :]
        high, low = halves(
            jnp.concatenate(
                [b[i * n_gx : (i + 1) * n_gx, :] for i in range(2) for b in blocks], axis=0
            )
        )
        for j in range(rows):
            cols = slice(j * LANES, (j + 1) * LANES)
            lanes = l_one[:, cols]
            found = nn_dot(high, lanes) + nn_dot(low, lanes)
            hits = t_one[:, cols].astype(F32)
            for i in range(2):
                sampled[i, j : j + 1, :] = jnp.sum(
                    found[i * owners : (i + 1) * owners, :] * hits, axis=0, keepdims=True
                )
        return sampled[0], sampled[1], sums

    def sum_a(partial):
        pb_send[...] = jnp.broadcast_to(partial, pb_send.shape)

        def body(k, _):
            gx_copy(pb_send, pb_recv.at[k], p_ss.at[0], p_rs.at[0], k, 1).start()
            return 0

        lax.fori_loop(1, n_gx, body, 0)
        pb_recv[0] = pb_send[...]

    def sum_b():
        wait_for(pb_recv.at[pl.ds(1, n_gx - 1)], p_rs.at[0])
        pa_send[...] = jnp.sum(pb_recv[...], axis=0)
        for k in range(1, n_gy):
            gy_copy(pa_send, pa_recv.at[k], p_ss.at[1], p_rs.at[1], k, 1).start()
        pa_recv[0] = pa_send[...]

    def sum_c():
        wait_for(pa_recv.at[pl.ds(1, n_gy - 1)], p_rs.at[1])
        return jnp.sum(pa_recv[...], axis=0)[0:1, :]

    live = lax.broadcasted_iota(jnp.int32, (rows, LANES), 0) < count[...]
    rhs = jnp.where(live, jump[...], 0.0)
    steady = stiff[...]
    sw = jnp.where(live, weight[...], 0.0)
    fields = [to_rows(cell[...], split_index)] + [to_rows(x, halves) for x in (rhs, steady, sw)]
    pl.semaphore_wait(barrier, n_gx + n_gy + 2)
    forward_a(fields)

    def place(x, _):
        for h in range(2):
            rim[DEPTH + x, h, EDGE : EDGE + size_y, :] = beta[x, :, h * LANES : (h + 1) * LANES]
        return 0

    lax.fori_loop(0, size_x, place, 0)
    rim_send(0)
    forward_b()

    def rows_at(ref, x, h, start, n):
        return ref[x, h, pl.ds(start, n), :]

    def z_sides(low, high, lane):
        low_up, high_up = pltpu.roll(low, 1, 1), pltpu.roll(high, 1, 1)
        low_dn, high_dn = pltpu.roll(low, LANES - 1, 1), pltpu.roll(high, LANES - 1, 1)
        return (
            (low_up, jnp.where(lane == 0, low_up, high_up)),
            (jnp.where(lane == LANES - 1, high_dn, low_dn), high_dn),
        )

    def harmonic(a, b):
        both = a + b
        return 2.0 * a * b / jnp.where(both > 0, both, 1.0)

    rim_wait(0)

    def coefficients(x, y):
        row = y + PAD
        centre = [rows_at(rim, x + 1, h, row, PAD) for h in range(2)]
        before, after = z_sides(centre[0], centre[1], lane8)
        for h in range(2):
            c = centre[h]
            kxl = harmonic(c, rows_at(rim, x, h, row, PAD))
            kxh = harmonic(c, rows_at(rim, x + 2, h, row, PAD))
            kyl = harmonic(c, rows_at(rim, x + 1, h, row - 1, PAD))
            kyh = harmonic(c, rows_at(rim, x + 1, h, row + 1, PAD))
            kzl = harmonic(c, before[h])
            kzh = harmonic(c, after[h])
            if h == 0:
                kzl = jnp.where(lane8 == 0, 0.0, kzl)
            else:
                kzh = jnp.where(lane8 == LANES - 1, 0.0, kzh)
            inverse = 1.0 / (SHIFT + kxl + kxh + kyl + kyh + kzl + kzh)
            at = (x, h, pl.ds(y, PAD), slice(None))
            invd[at] = inverse
            axl[at] = kxl * inverse
            axh[at] = kxh * inverse
            ayl[at] = kyl * inverse
            ayh[at] = kyh * inverse
            azl[at] = kzl * inverse
            azh[at] = kzh * inverse

    def coefficient_planes(i, _):
        for x in range(2):
            for y in range(0, size_y + 2 * PAD, PAD):
                coefficients(2 * i + x, y)
        return 0

    lax.fori_loop(0, planes // 2 - 1, coefficient_planes, 0)

    index, slot_rhs, slot_steady, slot_sw = forward_c()
    index = index.astype(jnp.int32) - 1
    z_at[...] = jnp.where(index < 0, -1, index & (size_z - 1))
    slot_val[...] = index >> 8
    iota_c = lax.broadcasted_iota(jnp.int32, (columns, LANES), 0)
    per = chunk // LANES
    iota_z = lax.broadcasted_iota(jnp.int32, (size_z, LANES), 0)
    for j in range(n_gx):
        row = slot_val[j : j + 1, :]
        c_one[:, j * LANES : (j + 1) * LANES] = jnp.where(row == iota_c, 1.0, 0.0).astype(BF16)

    def spread_grid(f, values):
        picked[...] = values
        for j in range(n_gx):
            row = picked[j : j + 1, :]
            hit = z_at[j : j + 1, :] == iota_z
            high = row.astype(BF16).astype(F32)
            cols = slice(j * LANES, (j + 1) * LANES)
            z_high[:, cols] = jnp.where(hit, high, 0.0).astype(BF16)
            z_low[:, cols] = jnp.where(hit, row - high, 0.0).astype(BF16)
        group = 4

        def body(i, _):
            cols = c_one[pl.ds(i * group * size_y, group * size_y), :]
            source = nt_dot(cols, z_high[...]) + nt_dot(cols, z_low[...])
            for q in range(group):
                x = i * group + q
                for h in range(2):
                    part = source[q * size_y : (q + 1) * size_y, h * LANES : (h + 1) * LANES]
                    rim[f * planes + DEPTH + x, h, EDGE : EDGE + size_y, :] = (
                        part * invd[DEPTH - 1 + x, h, PAD : PAD + size_y, :]
                    )
            return 0

        lax.fori_loop(0, size_x // group, body, 0)

    def sample_grid(p):
        def turn(x, _):
            for h in range(2):
                high, low = halves(u[p, DEPTH + x, h, EDGE : EDGE + size_y, :].T)
                field_t[x, h * LANES : (h + 1) * LANES, :] = high
                field_t[x, size_z + h * LANES : size_z + (h + 1) * LANES, :] = low
            return 0

        lax.fori_loop(0, size_x, turn, 0)
        whole = jnp.concatenate([field_t[x] for x in range(size_x)], axis=1)

        def body(i, _):
            found = nn_dot(whole, c_one[:, pl.ds(pl.multiple_of(i * chunk, LANES), chunk)])
            for q in range(per):
                j = i * per + q
                hit = z_at[pl.ds(j, 1), :] == iota_z
                cols = slice(q * LANES, (q + 1) * LANES)
                both = found[:size_z, cols] + found[size_z:, cols]
                picked[pl.ds(j, 1), :] = jnp.sum(
                    jnp.where(hit, both, 0.0), axis=0, keepdims=True
                )
            return 0

        lax.fori_loop(0, slots // chunk, body, 0)

    def relax(f, step, x, y, n, first, second):
        lane = lax.broadcasted_iota(jnp.int32, (n, LANES), 1)
        row = y + PAD

        def field(x, h, row):
            if step == 0:
                return rim[f * planes + x, h, pl.ds(row, n), :]
            return u[(step - 1) % 2, x, h, pl.ds(row, n), :]

        centre = [field(x, h, row) for h in range(2)]
        before, after = z_sides(centre[0], centre[1], lane)
        for h in range(2):
            at = (x - 1, h, pl.ds(y, n), slice(None))
            sides = axl[at] * field(x - 1, h, row) + axh[at] * field(x + 1, h, row)
            sides += ayl[at] * field(x, h, row - 1) + ayh[at] * field(x, h, row + 1)
            sides += azl[at] * before[h] + azh[at] * after[h]
            if step == 0:
                now = centre[h] * (1.0 / THETA)
                update = first * now + second * (centre[h] + (sides - centre[h]) * (1.0 / THETA))
            else:
                now = centre[h]
                update = first * d[at] + second * (rim[f * planes + x, h, pl.ds(row, n), :] + sides - now)
            d[at] = update
            u[step % 2, x, h, pl.ds(row, n), :] = now + update

    def pressure(f):
        rim_send(f)
        rim_wait(f)
        for step, (first, second) in enumerate(sweep_factors()):
            more = CHEB - 2 - step
            low, high = (0, size_y + 2 * PAD) if more else (PAD, size_y + PAD)
            count = size_x + 2 * more
            parts = PARTS if count % PARTS == 0 else 2

            def body(i, _):
                for q in range(count // parts):
                    x = DEPTH - more + i * (count // parts) + q
                    for y in range(low, high, (high - low) // 2):
                        relax(f, step, x, y, (high - low) // 2, first, second)
                return 0

            lax.fori_loop(0, parts, body, 0)
        return (CHEB - 2) % 2

    spread_grid(1, slot_sw * slot_rhs)
    sample_grid(pressure(1))
    got_1 = picked[...]
    slot_a = slot_steady * slot_rhs + slot_sw * got_1
    sum_a(pack_row([total(slot_rhs * slot_rhs), total(slot_rhs * slot_a)]))
    spread_grid(2, slot_sw * slot_a)
    sum_b()
    end = pressure(2)
    sum_bb, sum_ab = unpack_row(sum_c(), 2)
    sample_grid(end)
    got_2 = picked[...]
    start = jnp.sqrt(sum_bb + EPS)
    scale = 1.0 / start
    h_11 = sum_ab * scale * scale

    def basis(first, image, image_of_image):
        v_1 = first * scale
        w_1 = image * scale
        return v_1, w_1, w_1 - h_11 * v_1, image_of_image * scale - h_11 * w_1

    v_1, _, z, s_z = basis(slot_rhs, slot_a, slot_steady * slot_a + slot_sw * got_2)
    pairs = ((z, z), (s_z, v_1), (s_z, z), (s_z, s_z), (v_1, v_1), (v_1, z))
    back_a(got_1, got_2, pack_row([total(p * q) for p, q in pairs]))
    back_b()
    got_1, got_2, sums = back_c()
    image_1 = steady * rhs + sw * got_1
    v_1, w_1, z, s_z = basis(rhs, image_1, jnp.where(live, steady, 0.0) * image_1 + sw * got_2)
    zz, szv, szz, szsz, v1v1, v1z = unpack_row(sums, 6)
    h_21 = jnp.sqrt(zz + EPS)
    inverse = 1.0 / h_21
    v_2 = z * inverse
    w_2 = s_z * inverse
    w2v1, w2v2, w2w2 = szv * inverse, szz * inverse * inverse, szsz * inverse * inverse
    v1v2, v2v2 = v1z * inverse, zz * inverse * inverse
    h_12 = w2v1
    h_22 = w2v2 - h_12 * v1v2
    square = (
        w2w2
        + h_12 * h_12 * v1v1
        + h_22 * h_22 * v2v2
        - 2.0 * h_12 * w2v1
        - 2.0 * h_22 * w2v2
        + 2.0 * h_12 * h_22 * v1v2
    )
    h_32 = jnp.sqrt(jnp.maximum(square, 0.0) + EPS)
    y_1, y_2 = least_squares(start, [[h_11, h_21], [h_12, h_22, h_32]])
    sol[...] = y_1 * v_1 + y_2 * v_2
    res[...] = rhs - y_1 * w_1 - y_2 * w_2

    for f in range(3):
        rim_wait_sent(f)
    wait_for(fa_send.at[pl.ds(1, n_gy - 1)], a_ss.at[0])
    wait_for(ra_recv.at[pl.ds(1, n_gy - 1)], a_ss.at[1])
    wait_for(fb_send.at[pl.ds(1, n_gx - 1)], b_ss.at[0])
    wait_for(rb_send.at[pl.ds(1, n_gx - 1)], b_ss.at[1])
    wait_for(pb_recv.at[pl.ds(1, n_gx - 1)], p_ss.at[0])
    wait_for(pa_recv.at[pl.ds(1, n_gy - 1)], p_ss.at[1])


def on_device(n_gx, n_gy, beta, jump, stiff, weight, owner, cell, count):
    size_x, size_y, size_z = beta.shape
    points = jump.shape[0]
    rows = points // LANES
    owners = n_gx * n_gy
    columns = size_x * size_y
    planes = size_x + 2 * DEPTH
    wide = (planes, 2, size_y + 4 * PAD, LANES)
    tile = (planes - 2, 2, size_y + 2 * PAD, LANES)
    slots = n_gx * LANES
    dma = pltpu.SemaphoreType.DMA
    scratch = [
        pltpu.VMEM((owners, points), BF16),
        pltpu.VMEM((LANES, points), BF16),
        pltpu.VMEM((rows, LANES), jnp.int32),
        pltpu.VMEM((rows, LANES), jnp.int32),
        pltpu.VMEM((3 * planes,) + wide[1:], F32),
        pltpu.VMEM((2,) + wide, F32),
        pltpu.VMEM(tile, F32),
        pltpu.VMEM(tile, F32),
        pltpu.VMEM(tile, F32),
        pltpu.VMEM(tile, F32),
        pltpu.VMEM(tile, F32),
        pltpu.VMEM(tile, F32),
        pltpu.VMEM(tile, F32),
        pltpu.VMEM(tile, F32),
        pltpu.VMEM((size_x, 2 * size_z, size_y), BF16),
        pltpu.VMEM((columns, slots), BF16),
        pltpu.VMEM((size_z, slots), BF16),
        pltpu.VMEM((size_z, slots), BF16),
        pltpu.VMEM((n_gx, LANES), jnp.int32),
        pltpu.VMEM((n_gx, LANES), jnp.int32),
        pltpu.VMEM((n_gx, LANES), F32),
        pltpu.VMEM((2, rows, LANES), F32),
        pltpu.VMEM((n_gy, 4 * n_gx, LANES), F32),
        pltpu.VMEM((n_gy, 4 * n_gx, LANES), F32),
        pltpu.VMEM((n_gx, 4, LANES), F32),
        pltpu.VMEM((n_gx, 4, LANES), F32),
        pltpu.VMEM((n_gx, 4, LANES), F32),
        pltpu.VMEM((n_gx, 4, LANES), F32),
        pltpu.VMEM((2 * n_gx + PAD, LANES), F32),
        pltpu.VMEM((n_gy, 2 * n_gx + PAD, LANES), F32),
        pltpu.VMEM((2, LANES), F32),
        pltpu.VMEM((n_gx, 2, LANES), F32),
        pltpu.VMEM((2, LANES), F32),
        pltpu.VMEM((n_gy, 2, LANES), F32),
    ] + [dma((2,))] * 6 + [dma((3, len(SIDES)))] * 2
    vmem = pl.BlockSpec(memory_space=pltpu.VMEM)
    out = jax.ShapeDtypeStruct((rows, LANES), F32)
    solution, residual = pl.pallas_call(
        functools.partial(kernel, n_gx, n_gy),
        out_shape=(out, out),
        in_specs=[vmem] * 7,
        out_specs=(vmem, vmem),
        scratch_shapes=scratch,
        compiler_params=pltpu.CompilerParams(
            collective_id=0, has_side_effects=True, vmem_limit_bytes=56 * 1024 * 1024
        ),
    )(
        beta,
        jump.reshape(rows, LANES),
        stiff.reshape(rows, LANES),
        weight.reshape(rows, LANES),
        owner.reshape(rows, LANES),
        cell.reshape(rows, LANES),
        count.reshape(1, 1),
    )
    return solution.reshape(points), residual.reshape(points)


def solution(mesh):
    points = P(("gx", "gy"))
    return jax.shard_map(
        functools.partial(on_device, mesh.shape["gx"], mesh.shape["gy"]),
        mesh=mesh,
        in_specs=(P("gx", "gy", None), points, points, points, P(("gx", "gy"), None), points, points),
        out_specs=(points, points),
        check_vma=False,
    )
```

```python
import functools

import jax
import jax.numpy as jnp
from jax import lax
from jax.experimental import pallas as pl
from jax.experimental.pallas import tpu as pltpu
from jax.sharding import PartitionSpec as P

CHEB = 6
SHIFT = 0.01
THETA = 1.025
DELTA = 0.975
SIGMA = THETA / DELTA
EPS = 1e-06
LANES = 128
PAD = 8
EDGE = 2 * PAD
DEPTH = CHEB - 1
SIDES = [(x, y) for x in (-1, 0, 1) for y in (-1, 0, 1) if (x, y) != (0, 0)]
MESH = pl.DeviceIdType.MESH
F32 = jnp.float32
BF16 = jnp.bfloat16
CHUNK = 512


def sweep_factors():
    factors = []
    ratio = 1.0 / SIGMA
    for _ in range(CHEB - 1):
        ratio_next = 1.0 / (2.0 * SIGMA - ratio)
        factors.append((ratio_next * ratio, 2.0 * ratio_next / DELTA))
        ratio = ratio_next
    return factors


def least_squares(start, columns):
    count = len(columns)
    targets = [start] + [start * 0.0 for unused in range(count)]
    cosines = []
    sines = []
    upper = []
    for outer in range(count):
        column = list(columns[outer])
        for inner in range(outer):
            first = cosines[inner] * column[inner] + sines[inner] * column[inner + 1]
            second = -sines[inner] * column[inner] + cosines[inner] * column[inner + 1]
            column[inner] = first
            column[inner + 1] = second
        radius = jnp.sqrt(column[outer] * column[outer] + column[outer + 1] * column[outer + 1])
        cosine = column[outer] / radius
        sine = column[outer + 1] / radius
        column[outer] = radius
        targets[outer + 1] = -sine * targets[outer]
        targets[outer] = cosine * targets[outer]
        cosines.append(cosine)
        sines.append(sine)
        upper.append(column)
    coeffs = [None] * count
    for outer in reversed(range(count)):
        total = targets[outer]
        for later in range(outer + 1, count):
            total = total - upper[later][outer] * coeffs[later]
        coeffs[outer] = total / upper[outer][outer]
    return coeffs


def halves(x):
    high = x.astype(BF16)
    low = (x - high.astype(F32)).astype(BF16)
    return high, low


def nt_dot(a, b):
    return lax.dot_general(a, b, (((1,), (1,)), ((), ())), preferred_element_type=F32)


def nn_dot(a, b):
    return lax.dot_general(a, b, (((1,), (0,)), ((), ())), preferred_element_type=F32)


def total(x):
    return jnp.sum(jnp.sum(x, axis=0, keepdims=True), axis=1, keepdims=True)


def pack_row(values):
    lane = lax.broadcasted_iota(jnp.int32, (1, LANES), 1)
    row = jnp.zeros((1, LANES), F32)
    for at, value in enumerate(values):
        row = jnp.where(lane == at, value, row)
    return row


def unpack_row(row, count):
    lane = lax.broadcasted_iota(jnp.int32, (1, LANES), 1)
    return [
        jnp.sum(jnp.where(lane == at, row, 0.0), axis=1, keepdims=True) for at in range(count)
    ]


def kernel(
    n_gx,
    n_gy,
    beta,
    jump,
    stiff,
    weight,
    owner,
    cell,
    count,
    sol,
    res,
    t_one,
    l_one,
    target,
    lanes_at,
    rim,
    u,
    d,
    invd,
    axl,
    axh,
    ayl,
    ayh,
    azl,
    azh,
    field_c,
    field_t,
    c_one,
    z_both,
    z_at,
    slot_val,
    picked,
    sampled,
    fa_send,
    fa_recv,
    fb_send,
    fb_recv,
    rb_send,
    rb_recv,
    ra_send,
    ra_recv,
    pb_send,
    pb_recv,
    pa_send,
    pa_recv,
    a_ss,
    a_rs,
    b_ss,
    b_rs,
    p_ss,
    p_rs,
    rim_ss,
    rim_rs,
):
    me_x = lax.axis_index("gx")
    me_y = lax.axis_index("gy")
    size_x, size_y, size_z = beta.shape
    rows = jump.shape[0]
    points = rows * LANES
    owners = n_gx * n_gy
    cap = LANES // n_gy
    slots = n_gx * LANES
    columns = size_x * size_y
    chunk = min(CHUNK, slots)
    lane8 = lax.broadcasted_iota(jnp.int32, (PAD, LANES), 1)

    def at_gx(shift):
        return {"gx": lax.rem(me_x + shift + n_gx, n_gx), "gy": me_y}

    def at_gy(shift):
        return {"gx": me_x, "gy": lax.rem(me_y + shift + n_gy, n_gy)}

    planes = size_x + 2 * DEPTH

    def clear_planes(first):
        for f in range(3):
            for x in range(DEPTH):
                at = f * planes + first + x
                rim[at] = jnp.zeros(rim.shape[1:], F32)

    def clear_rows(first):
        def body(x, _):
            rim[x, :, first : first + EDGE, :] = jnp.zeros((2, EDGE, LANES), F32)
            return 0

        lax.fori_loop(0, rim.shape[0], body, 0)

    pl.when(me_x == 0)(lambda: clear_planes(0))
    pl.when(me_x == n_gx - 1)(lambda: clear_planes(size_x + DEPTH))
    pl.when(me_y == 0)(lambda: clear_rows(0))
    pl.when(me_y == n_gy - 1)(lambda: clear_rows(EDGE + size_y))

    barrier = pltpu.get_barrier_semaphore()

    def greet_x(k, _):
        pl.semaphore_signal(barrier, inc=1, device_id=at_gx(k), device_id_type=MESH)
        return 0

    def greet_y(k, _):
        pl.semaphore_signal(barrier, inc=1, device_id=at_gy(k), device_id_type=MESH)
        return 0

    lax.fori_loop(1, n_gx, greet_x, 0)
    lax.fori_loop(1, n_gy, greet_y, 0)
    for side_x, side_y in SIDES:
        if side_x * side_y:
            corner = {"gx": at_gx(side_x)["gx"], "gy": at_gy(side_y)["gy"]}
            pl.semaphore_signal(barrier, inc=1, device_id=corner, device_id_type=MESH)

    def gx_copy(src, dst, send, recv, k, sign):
        return pltpu.make_async_remote_copy(
            src_ref=src,
            dst_ref=dst,
            send_sem=send,
            recv_sem=recv,
            device_id=at_gx(sign * k),
            device_id_type=MESH,
        )

    def gy_copy(src, dst, send, recv, k, sign):
        return pltpu.make_async_remote_copy(
            src_ref=src,
            dst_ref=dst,
            send_sem=send,
            recv_sem=recv,
            device_id=at_gy(sign * k),
            device_id_type=MESH,
        )

    def wait_for(ref, sem):
        pltpu.make_async_copy(ref, ref, sem).wait()

    def send_gx(src, dst, send, recv, sign):
        def body(k, _):
            gx_copy(src.at[k], dst.at[k], send, recv, k, sign).start()
            return 0

        lax.fori_loop(1, n_gx, body, 0)

    def inside(x, y):
        return (x >= 0) & (x < n_gx) & (y >= 0) & (y < n_gy)

    def rim_copies(f):
        span_x = {
            -1: (DEPTH, DEPTH + size_x, DEPTH),
            0: (DEPTH, DEPTH, size_x),
            1: (size_x, 0, DEPTH),
        }
        span_y = {
            -1: (EDGE, EDGE + size_y, PAD),
            0: (EDGE, EDGE, size_y),
            1: (EDGE + size_y - PAD, EDGE - PAD, PAD),
        }
        for i, (side_x, side_y) in enumerate(SIDES):
            def copy(i=i, side_x=side_x, side_y=side_y, x=span_x[side_x], y=span_y[side_y]):
                return pltpu.make_async_remote_copy(
                    src_ref=rim_part(f, x[0], x[2], y[0], y[2]),
                    dst_ref=rim_part(f, x[1], x[2], y[1], y[2]),
                    send_sem=rim_ss.at[f, i],
                    recv_sem=rim_rs.at[f, i],
                    device_id={"gx": at_gx(side_x)["gx"], "gy": at_gy(side_y)["gy"]},
                    device_id_type=MESH,
                )

            yield (
                inside(me_x + side_x, me_y + side_y),
                inside(me_x - side_x, me_y - side_y),
                copy,
            )

    def rim_part(f, x, count_x, y, count_y):
        return rim.at[pl.ds(f * planes + x, count_x), :, pl.ds(y, count_y), :]

    def rim_send(f, along_x=(True, False)):
        for (side_x, _), (sent, _, copy) in zip(SIDES, rim_copies(f)):
            if (side_x != 0) in along_x:
                pl.when(sent)(lambda: copy().start())

    def rim_wait(f, along_x=(True, False)):
        for (side_x, _), (_, received, copy) in zip(SIDES, rim_copies(f)):
            if (side_x != 0) in along_x:
                pl.when(received)(lambda: copy().wait_recv())

    def rim_wait_sent(f):
        for sent, _, copy in rim_copies(f):
            pl.when(sent)(lambda: copy().wait_send())

    def place(x, _):
        for h in range(2):
            rim[DEPTH + x, h, EDGE : EDGE + size_y, :] = beta[x, :, h * LANES : (h + 1) * LANES]
        return 0

    lax.fori_loop(0, size_x, place, 0)

    shift_gy = n_gy.bit_length() - 1
    own = owner[...]
    target[...] = ((own & (n_gy - 1)) - me_y & (n_gy - 1)) * n_gx + (
        (own >> shift_gy) - me_x & (n_gx - 1)
    )
    iota_t = lax.broadcasted_iota(jnp.int32, (owners, LANES), 0)
    iota_l = lax.broadcasted_iota(jnp.int32, (LANES, LANES), 0)
    above = lax.broadcasted_iota(jnp.int32, (LANES, 2 * LANES), 1)
    below = lax.broadcasted_iota(jnp.int32, (LANES, 2 * LANES), 0)
    counter = ((below < above) | (above >= LANES)).astype(BF16)
    offset = jnp.zeros((owners, LANES), F32)
    for j in range(rows):
        hit = target[j : j + 1, :] == iota_t
        hit_f = jnp.where(hit, 1.0, 0.0)
        hit_b = hit_f.astype(BF16)
        t_one[:, j * LANES : (j + 1) * LANES] = hit_b
        both = nn_dot(hit_b, counter)
        rank = jnp.sum(hit_f * (both[:, :LANES] + offset), axis=0, keepdims=True)
        offset = offset + both[:, LANES:]
        lane_of = rank.astype(jnp.int32) + me_y * cap
        l_one[:, j * LANES : (j + 1) * LANES] = jnp.where(lane_of == iota_l, 1.0, 0.0).astype(BF16)

    def to_rows(vector, row_of):
        out = jnp.zeros((owners, LANES), F32)
        for j in range(rows):
            cols = slice(j * LANES, (j + 1) * LANES)
            for part in row_of(vector[j : j + 1, :]):
                spread = t_one[:, cols] * part
                out = out + nt_dot(spread, l_one[:, cols])
        return out

    def split_index(row):
        low = (row & (2 * LANES - 1)) + 1
        middle = (row >> 8) & (2 * LANES - 1)
        high = row >> 16
        return [
            x.astype(F32).astype(BF16) for x in (low, middle * 256, high * 65536)
        ]

    def forward_a(fields):
        for k in range(n_gy):
            for i, field in enumerate(fields):
                fa_send[k, i * n_gx : (i + 1) * n_gx, :] = field[k * n_gx : (k + 1) * n_gx, :]
        for k in range(1, n_gy):
            gy_copy(fa_send.at[k], fa_recv.at[k], a_ss.at[0], a_rs.at[0], k, 1).start()

    def forward_b():
        wait_for(fa_recv.at[pl.ds(1, n_gy - 1)], a_rs.at[0])
        both = fa_send[0]
        for k in range(1, n_gy):
            both = both + fa_recv[k]
        for k in range(n_gx):
            for i in range(4):
                fb_send[k, i : i + 1, :] = both[i * n_gx + k : i * n_gx + k + 1, :]
        send_gx(fb_send, fb_recv, b_ss.at[0], b_rs.at[0], 1)
        fb_recv[0] = fb_send[0]

    def forward_c():
        wait_for(fb_recv.at[pl.ds(1, n_gx - 1)], b_rs.at[0])
        return [fb_recv[:, i, :] for i in range(4)]

    def back_a(first, second, sums):
        for k in range(n_gx):
            rb_send[k, 0:1, :] = first[k : k + 1, :]
            rb_send[k, 1:2, :] = second[k : k + 1, :]
            rb_send[k, 2:3, :] = sums
            rb_send[k, 3:4, :] = sums
        send_gx(rb_send, rb_recv, b_ss.at[1], b_rs.at[1], -1)
        rb_recv[0] = rb_send[0]

    def back_b():
        wait_for(rb_recv.at[pl.ds(1, n_gx - 1)], b_rs.at[1])
        ra_send[0:n_gx, :] = rb_recv[:, 0, :]
        ra_send[n_gx : 2 * n_gx, :] = rb_recv[:, 1, :]
        sums = jnp.sum(rb_recv[:, 2, :], axis=0, keepdims=True)
        ra_send[2 * n_gx : 2 * n_gx + PAD, :] = jnp.broadcast_to(sums, (PAD, LANES))
        for k in range(1, n_gy):
            gy_copy(ra_send, ra_recv.at[k], a_ss.at[1], a_rs.at[1], k, -1).start()

    def back_c():
        wait_for(ra_recv.at[pl.ds(1, n_gy - 1)], a_rs.at[1])
        blocks = [ra_send[...]] + [ra_recv[k] for k in range(1, n_gy)]
        sums = blocks[0][2 * n_gx : 2 * n_gx + 1, :]
        for b in blocks[1:]:
            sums = sums + b[2 * n_gx : 2 * n_gx + 1, :]
        high, low = halves(
            jnp.concatenate(
                [b[i * n_gx : (i + 1) * n_gx, :] for i in range(2) for b in blocks], axis=0
            )
        )
        for j in range(rows):
            cols = slice(j * LANES, (j + 1) * LANES)
            lanes = l_one[:, cols]
            found = nn_dot(high, lanes) + nn_dot(low, lanes)
            hits = t_one[:, cols].astype(F32)
            for i in range(2):
                sampled[i, j : j + 1, :] = jnp.sum(
                    found[i * owners : (i + 1) * owners, :] * hits, axis=0, keepdims=True
                )
        return sampled[0], sampled[1], sums

    def sum_a(partial):
        pb_send[...] = jnp.broadcast_to(partial, pb_send.shape)

        def body(k, _):
            gx_copy(pb_send, pb_recv.at[k], p_ss.at[0], p_rs.at[0], k, 1).start()
            return 0

        lax.fori_loop(1, n_gx, body, 0)
        pb_recv[0] = pb_send[...]

    def sum_b():
        wait_for(pb_recv.at[pl.ds(1, n_gx - 1)], p_rs.at[0])
        pa_send[...] = jnp.sum(pb_recv[...], axis=0)
        for k in range(1, n_gy):
            gy_copy(pa_send, pa_recv.at[k], p_ss.at[1], p_rs.at[1], k, 1).start()
        pa_recv[0] = pa_send[...]

    def sum_c():
        wait_for(pa_recv.at[pl.ds(1, n_gy - 1)], p_rs.at[1])
        return jnp.sum(pa_recv[...], axis=0)[0:1, :]

    live = lax.broadcasted_iota(jnp.int32, (rows, LANES), 0) < count[...]
    rhs = jnp.where(live, jump[...], 0.0)
    steady = stiff[...]
    sw = jnp.where(live, weight[...], 0.0)
    pl.semaphore_wait(barrier, n_gx + n_gy + 2)
    rim_send(0)
    fields = [to_rows(cell[...], split_index)] + [to_rows(x, halves) for x in (rhs, steady, sw)]
    forward_a(fields)

    def rows_at(ref, x, h, start, n):
        return ref[x, h, pl.ds(start, n), :]

    def z_sides(low, high, lane):
        low_up, high_up = pltpu.roll(low, 1, 1), pltpu.roll(high, 1, 1)
        low_dn, high_dn = pltpu.roll(low, LANES - 1, 1), pltpu.roll(high, LANES - 1, 1)
        return (
            (low_up, jnp.where(lane == 0, low_up, high_up)),
            (jnp.where(lane == LANES - 1, high_dn, low_dn), high_dn),
        )

    def harmonic(a, b):
        both = a + b
        return 2.0 * a * b / jnp.where(both > 0, both, 1.0)

    rim_wait(0)

    def coefficients(x, y):
        row = y + PAD
        centre = [rows_at(rim, x + 1, h, row, PAD) for h in range(2)]
        before, after = z_sides(centre[0], centre[1], lane8)
        for h in range(2):
            c = centre[h]
            kxl = harmonic(c, rows_at(rim, x, h, row, PAD))
            kxh = harmonic(c, rows_at(rim, x + 2, h, row, PAD))
            kyl = harmonic(c, rows_at(rim, x + 1, h, row - 1, PAD))
            kyh = harmonic(c, rows_at(rim, x + 1, h, row + 1, PAD))
            kzl = harmonic(c, before[h])
            kzh = harmonic(c, after[h])
            if h == 0:
                kzl = jnp.where(lane8 == 0, 0.0, kzl)
            else:
                kzh = jnp.where(lane8 == LANES - 1, 0.0, kzh)
            inverse = 1.0 / (SHIFT + kxl + kxh + kyl + kyh + kzl + kzh)
            at = (x, h, pl.ds(y, PAD), slice(None))
            invd[at] = inverse
            axl[at] = kxl * inverse
            axh[at] = kxh * inverse
            ayl[at] = kyl * inverse
            ayh[at] = kyh * inverse
            azl[at] = kzl * inverse
            azh[at] = kzh * inverse

    def coefficient_planes(i, _):
        for x in range(2):
            for y in range(0, size_y + 2 * PAD, PAD):
                coefficients(2 * i + x, y)
        return 0

    half = (planes // 2 - 1) // 2
    lax.fori_loop(0, half, coefficient_planes, 0)
    forward_b()
    lax.fori_loop(half, planes // 2 - 1, coefficient_planes, 0)

    index, slot_rhs, slot_steady, slot_sw = forward_c()
    index = index.astype(jnp.int32) - 1
    z_at[...] = jnp.where(index < 0, -1, index & (size_z - 1))
    slot_val[...] = index >> 8
    near = list(range(DEPTH)) + list(range(size_x - DEPTH, size_x))
    middle = range(DEPTH, size_x - DEPTH)
    runs = [
        [(x, 0, size_y) for x in near[:DEPTH]],
        [(x, 0, size_y) for x in near[DEPTH:]],
        [(x, y, PAD) for x in middle for y in (0, size_y - PAD)],
        [(x, PAD, size_y - 2 * PAD) for x in middle],
    ]
    iota_c = jnp.concatenate(
        [
            lax.broadcasted_iota(jnp.int32, (n, LANES), 0) + (x * size_y + y)
            for group in runs
            for x, y, n in group
        ],
        axis=0,
    )
    per = chunk // LANES
    iota_z = lax.broadcasted_iota(jnp.int32, (size_z, LANES), 0)
    for j in range(n_gx):
        row = slot_val[j : j + 1, :]
        c_one[:, j * LANES : (j + 1) * LANES] = jnp.where(row == iota_c, 1.0, 0.0).astype(BF16)

    def spread_grid(f, values):
        picked[...] = values
        for j in range(n_gx):
            row = picked[j : j + 1, :]
            hit = z_at[j : j + 1, :] == iota_z
            high = row.astype(BF16).astype(F32)
            cols = slice(j * LANES, (j + 1) * LANES)
            z_both[:size_z, cols] = jnp.where(hit, high, 0.0).astype(BF16)
            z_both[size_z:, cols] = jnp.where(hit, row - high, 0.0).astype(BF16)
        at = 0
        for i, group in enumerate(runs):
            count = sum(n for _, _, n in group)
            found = nt_dot(c_one[at : at + count, :], z_both[...])
            source = found[:, :size_z] + found[:, size_z:]
            at += count
            row = 0
            for x, y, n in group:
                for h in range(2):
                    rim[f * planes + DEPTH + x, h, EDGE + y : EDGE + y + n, :] = (
                        source[row : row + n, h * LANES : (h + 1) * LANES]
                        * invd[DEPTH - 1 + x, h, PAD + y : PAD + y + n, :]
                    )
                row += n
            if i == 1:
                rim_send(f, (True,))
            if i == 2:
                rim_send(f, (False,))

    def sample_grid(p):
        at = 0
        for group in runs:
            for x, y, n in group:
                for h in range(2):
                    field_c[at : at + n, h * LANES : (h + 1) * LANES] = u[
                        p, DEPTH + x, h, EDGE + y : EDGE + y + n, :
                    ]
                at += n
        for i in range(columns // LANES):
            cols = slice(i * LANES, (i + 1) * LANES)
            for h in range(2):
                high, low = halves(field_c[cols, h * LANES : (h + 1) * LANES].T)
                field_t[h * LANES : (h + 1) * LANES, cols] = high
                field_t[size_z + h * LANES : size_z + (h + 1) * LANES, cols] = low

        def body(i, _):
            found = nn_dot(
                field_t[...], c_one[:, pl.ds(pl.multiple_of(i * chunk, LANES), chunk)]
            )
            for q in range(per):
                j = i * per + q
                hit = z_at[pl.ds(j, 1), :] == iota_z
                cols = slice(q * LANES, (q + 1) * LANES)
                both = found[:size_z, cols] + found[size_z:, cols]
                picked[pl.ds(j, 1), :] = jnp.sum(
                    jnp.where(hit, both, 0.0), axis=0, keepdims=True
                )
            return 0

        lax.fori_loop(0, slots // chunk, body, 0)

    def relax(f, step, x, y, n, first, second):
        lane = lax.broadcasted_iota(jnp.int32, (n, LANES), 1)
        row = y + PAD

        def field(x, h, row):
            if step == 0:
                return rim[f * planes + x, h, pl.ds(row, n), :]
            return u[(step - 1) % 2, x, h, pl.ds(row, n), :]

        centre = [field(x, h, row) for h in range(2)]
        before, after = z_sides(centre[0], centre[1], lane)
        for h in range(2):
            at = (x - 1, h, pl.ds(y, n), slice(None))
            sides = axl[at] * field(x - 1, h, row) + axh[at] * field(x + 1, h, row)
            sides += ayl[at] * field(x, h, row - 1) + ayh[at] * field(x, h, row + 1)
            sides += azl[at] * before[h] + azh[at] * after[h]
            if step == 0:
                now = centre[h] * (1.0 / THETA)
                update = first * now + second * (centre[h] + (sides - centre[h]) * (1.0 / THETA))
            else:
                now = centre[h]
                update = first * d[at] + second * (rim[f * planes + x, h, pl.ds(row, n), :] + sides - now)
            d[at] = update
            u[step % 2, x, h, pl.ds(row, n), :] = now + update

    def pressure(f):
        rim_wait(f, (False,))
        factors = sweep_factors()

        def step_planes(step, start, count):
            low, high = (0, size_y + 2 * PAD) if step < CHEB - 2 else (PAD, size_y + PAD)
            n = (high - low) // 2
            for x in range(count):
                for y in (low, low + n):
                    relax(f, step, start + x, y, n, *factors[step])

        for step in range(CHEB - 1):
            step_planes(step, DEPTH + step + 1, size_x - 2 * (step + 1))
        rim_wait(f, (True,))
        for step in range(CHEB - 1):

            def body(side, _):
                step_planes(step, step + 1 + side * (planes - DEPTH - 2 * (step + 1)), DEPTH)
                return 0

            lax.fori_loop(0, 2, body, 0)
        return (CHEB - 2) % 2

    spread_grid(1, slot_sw * slot_rhs)
    sample_grid(pressure(1))
    got_1 = picked[...]
    slot_a = slot_steady * slot_rhs + slot_sw * got_1
    sum_a(pack_row([total(slot_rhs * slot_rhs), total(slot_rhs * slot_a)]))
    spread_grid(2, slot_sw * slot_a)
    sum_b()
    end = pressure(2)
    sum_bb, sum_ab = unpack_row(sum_c(), 2)
    sample_grid(end)
    got_2 = picked[...]
    start = jnp.sqrt(sum_bb + EPS)
    scale = 1.0 / start
    h_11 = sum_ab * scale * scale

    def basis(first, image, image_of_image):
        v_1 = first * scale
        w_1 = image * scale
        return v_1, w_1, w_1 - h_11 * v_1, image_of_image * scale - h_11 * w_1

    v_1, _, z, s_z = basis(slot_rhs, slot_a, slot_steady * slot_a + slot_sw * got_2)
    pairs = ((z, z), (s_z, v_1), (s_z, z), (s_z, s_z), (v_1, v_1), (v_1, z))
    back_a(got_1, got_2, pack_row([total(p * q) for p, q in pairs]))
    back_b()
    got_1, got_2, sums = back_c()
    image_1 = steady * rhs + sw * got_1
    v_1, w_1, z, s_z = basis(rhs, image_1, jnp.where(live, steady, 0.0) * image_1 + sw * got_2)
    zz, szv, szz, szsz, v1v1, v1z = unpack_row(sums, 6)
    h_21 = jnp.sqrt(zz + EPS)
    inverse = 1.0 / h_21
    v_2 = z * inverse
    w_2 = s_z * inverse
    w2v1, w2v2, w2w2 = szv * inverse, szz * inverse * inverse, szsz * inverse * inverse
    v1v2, v2v2 = v1z * inverse, zz * inverse * inverse
    h_12 = w2v1
    h_22 = w2v2 - h_12 * v1v2
    square = (
        w2w2
        + h_12 * h_12 * v1v1
        + h_22 * h_22 * v2v2
        - 2.0 * h_12 * w2v1
        - 2.0 * h_22 * w2v2
        + 2.0 * h_12 * h_22 * v1v2
    )
    h_32 = jnp.sqrt(jnp.maximum(square, 0.0) + EPS)
    y_1, y_2 = least_squares(start, [[h_11, h_21], [h_12, h_22, h_32]])
    sol[...] = y_1 * v_1 + y_2 * v_2
    res[...] = rhs - y_1 * w_1 - y_2 * w_2

    for f in range(3):
        rim_wait_sent(f)
    wait_for(fa_send.at[pl.ds(1, n_gy - 1)], a_ss.at[0])
    wait_for(ra_recv.at[pl.ds(1, n_gy - 1)], a_ss.at[1])
    wait_for(fb_send.at[pl.ds(1, n_gx - 1)], b_ss.at[0])
    wait_for(rb_send.at[pl.ds(1, n_gx - 1)], b_ss.at[1])
    wait_for(pb_recv.at[pl.ds(1, n_gx - 1)], p_ss.at[0])
    wait_for(pa_recv.at[pl.ds(1, n_gy - 1)], p_ss.at[1])


def on_device(n_gx, n_gy, beta, jump, stiff, weight, owner, cell, count):
    size_x, size_y, size_z = beta.shape
    points = jump.shape[0]
    rows = points // LANES
    owners = n_gx * n_gy
    columns = size_x * size_y
    planes = size_x + 2 * DEPTH
    wide = (planes, 2, size_y + 4 * PAD, LANES)
    tile = (planes - 2, 2, size_y + 2 * PAD, LANES)
    slots = n_gx * LANES
    dma = pltpu.SemaphoreType.DMA
    scratch = [
        pltpu.VMEM((owners, points), BF16),
        pltpu.VMEM((LANES, points), BF16),
        pltpu.VMEM((rows, LANES), jnp.int32),
        pltpu.VMEM((rows, LANES), jnp.int32),
        pltpu.VMEM((3 * planes,) + wide[1:], F32),
        pltpu.VMEM((2,) + wide, F32),
        pltpu.VMEM(tile, F32),
        pltpu.VMEM(tile, F32),
        pltpu.VMEM(tile, F32),
        pltpu.VMEM(tile, F32),
        pltpu.VMEM(tile, F32),
        pltpu.VMEM(tile, F32),
        pltpu.VMEM(tile, F32),
        pltpu.VMEM(tile, F32),
        pltpu.VMEM((columns, size_z), F32),
        pltpu.VMEM((2 * size_z, columns), BF16),
        pltpu.VMEM((columns, slots), BF16),
        pltpu.VMEM((2 * size_z, slots), BF16),
        pltpu.VMEM((n_gx, LANES), jnp.int32),
        pltpu.VMEM((n_gx, LANES), jnp.int32),
        pltpu.VMEM((n_gx, LANES), F32),
        pltpu.VMEM((2, rows, LANES), F32),
        pltpu.VMEM((n_gy, 4 * n_gx, LANES), F32),
        pltpu.VMEM((n_gy, 4 * n_gx, LANES), F32),
        pltpu.VMEM((n_gx, 4, LANES), F32),
        pltpu.VMEM((n_gx, 4, LANES), F32),
        pltpu.VMEM((n_gx, 4, LANES), F32),
        pltpu.VMEM((n_gx, 4, LANES), F32),
        pltpu.VMEM((2 * n_gx + PAD, LANES), F32),
        pltpu.VMEM((n_gy, 2 * n_gx + PAD, LANES), F32),
        pltpu.VMEM((2, LANES), F32),
        pltpu.VMEM((n_gx, 2, LANES), F32),
        pltpu.VMEM((2, LANES), F32),
        pltpu.VMEM((n_gy, 2, LANES), F32),
    ] + [dma((2,))] * 6 + [dma((3, len(SIDES)))] * 2
    vmem = pl.BlockSpec(memory_space=pltpu.VMEM)
    out = jax.ShapeDtypeStruct((rows, LANES), F32)
    solution, residual = pl.pallas_call(
        functools.partial(kernel, n_gx, n_gy),
        out_shape=(out, out),
        in_specs=[vmem] * 7,
        out_specs=(vmem, vmem),
        scratch_shapes=scratch,
        compiler_params=pltpu.CompilerParams(
            collective_id=0, has_side_effects=True, vmem_limit_bytes=56 * 1024 * 1024
        ),
    )(
        beta,
        jump.reshape(rows, LANES),
        stiff.reshape(rows, LANES),
        weight.reshape(rows, LANES),
        owner.reshape(rows, LANES),
        cell.reshape(rows, LANES),
        count.reshape(1, 1),
    )
    return solution.reshape(points), residual.reshape(points)


def solution(mesh):
    points = P(("gx", "gy"))
    return jax.shard_map(
        functools.partial(on_device, mesh.shape["gx"], mesh.shape["gy"]),
        mesh=mesh,
        in_specs=(P("gx", "gy", None), points, points, points, P(("gx", "gy"), None), points, points),
        out_specs=(points, points),
        check_vma=False,
    )
```

```python
import functools

import jax
import jax.numpy as jnp
from jax import lax
from jax.experimental import pallas as pl
from jax.experimental.pallas import tpu as pltpu
from jax.sharding import PartitionSpec as P

CHEB = 6
SHIFT = 0.01
THETA = 1.025
DELTA = 0.975
SIGMA = THETA / DELTA
EPS = 1e-06
LANES = 128
PAD = 8
EDGE = 2 * PAD
DEPTH = CHEB - 1
SIDES = [(x, y) for x in (-1, 0, 1) for y in (-1, 0, 1) if (x, y) != (0, 0)]
MESH = pl.DeviceIdType.MESH
F32 = jnp.float32
BF16 = jnp.bfloat16
CHUNK = 1024


def sweep_factors():
    factors = []
    ratio = 1.0 / SIGMA
    for _ in range(CHEB - 1):
        ratio_next = 1.0 / (2.0 * SIGMA - ratio)
        factors.append((ratio_next * ratio, 2.0 * ratio_next / DELTA))
        ratio = ratio_next
    return factors


def least_squares(start, columns):
    count = len(columns)
    targets = [start] + [start * 0.0 for unused in range(count)]
    cosines = []
    sines = []
    upper = []
    for outer in range(count):
        column = list(columns[outer])
        for inner in range(outer):
            first = cosines[inner] * column[inner] + sines[inner] * column[inner + 1]
            second = -sines[inner] * column[inner] + cosines[inner] * column[inner + 1]
            column[inner] = first
            column[inner + 1] = second
        radius = jnp.sqrt(column[outer] * column[outer] + column[outer + 1] * column[outer + 1])
        cosine = column[outer] / radius
        sine = column[outer + 1] / radius
        column[outer] = radius
        targets[outer + 1] = -sine * targets[outer]
        targets[outer] = cosine * targets[outer]
        cosines.append(cosine)
        sines.append(sine)
        upper.append(column)
    coeffs = [None] * count
    for outer in reversed(range(count)):
        total = targets[outer]
        for later in range(outer + 1, count):
            total = total - upper[later][outer] * coeffs[later]
        coeffs[outer] = total / upper[outer][outer]
    return coeffs


def halves(x):
    high = x.astype(BF16)
    low = (x - high.astype(F32)).astype(BF16)
    return high, low


def nt_dot(a, b):
    return lax.dot_general(a, b, (((1,), (1,)), ((), ())), preferred_element_type=F32)


def nn_dot(a, b):
    return lax.dot_general(a, b, (((1,), (0,)), ((), ())), preferred_element_type=F32)


def total(x):
    return jnp.sum(jnp.sum(x, axis=0, keepdims=True), axis=1, keepdims=True)


def pack_row(values):
    lane = lax.broadcasted_iota(jnp.int32, (1, LANES), 1)
    row = jnp.zeros((1, LANES), F32)
    for at, value in enumerate(values):
        row = jnp.where(lane == at, value, row)
    return row


def unpack_row(row, count):
    lane = lax.broadcasted_iota(jnp.int32, (1, LANES), 1)
    return [
        jnp.sum(jnp.where(lane == at, row, 0.0), axis=1, keepdims=True) for at in range(count)
    ]


def kernel(
    n_gx,
    n_gy,
    beta,
    jump,
    stiff,
    weight,
    owner,
    cell,
    count,
    sol,
    res,
    t_one,
    l_one,
    target,
    lanes_at,
    rim,
    u,
    d,
    invd,
    axl,
    axh,
    ayl,
    ayh,
    azl,
    azh,
    field_c,
    field_t,
    c_one,
    z_both,
    z_at,
    slot_val,
    picked,
    sampled,
    fa_send,
    fa_recv,
    fb_send,
    fb_recv,
    rb_send,
    rb_recv,
    ra_send,
    ra_recv,
    pb_send,
    pb_recv,
    pa_send,
    pa_recv,
    a_ss,
    a_rs,
    b_ss,
    b_rs,
    p_ss,
    p_rs,
    rim_ss,
    rim_rs,
):
    me_x = lax.axis_index("gx")
    me_y = lax.axis_index("gy")
    size_x, size_y, size_z = beta.shape
    rows = jump.shape[0]
    points = rows * LANES
    owners = n_gx * n_gy
    cap = LANES // n_gy
    slots = n_gx * LANES
    columns = size_x * size_y
    chunk = min(CHUNK, slots)
    lane8 = lax.broadcasted_iota(jnp.int32, (PAD, LANES), 1)

    def at_gx(shift):
        return {"gx": lax.rem(me_x + shift + n_gx, n_gx), "gy": me_y}

    def at_gy(shift):
        return {"gx": me_x, "gy": lax.rem(me_y + shift + n_gy, n_gy)}

    planes = size_x + 2 * DEPTH

    def clear_planes(first):
        for f in range(3):
            for x in range(DEPTH):
                at = f * planes + first + x
                rim[at] = jnp.zeros(rim.shape[1:], F32)

    def clear_rows(first):
        def body(x, _):
            rim[x, :, first : first + EDGE, :] = jnp.zeros((2, EDGE, LANES), F32)
            return 0

        lax.fori_loop(0, rim.shape[0], body, 0)

    pl.when(me_x == 0)(lambda: clear_planes(0))
    pl.when(me_x == n_gx - 1)(lambda: clear_planes(size_x + DEPTH))
    pl.when(me_y == 0)(lambda: clear_rows(0))
    pl.when(me_y == n_gy - 1)(lambda: clear_rows(EDGE + size_y))

    barrier = pltpu.get_barrier_semaphore()

    def greet_x(k, _):
        pl.semaphore_signal(barrier, inc=1, device_id=at_gx(k), device_id_type=MESH)
        return 0

    def greet_y(k, _):
        pl.semaphore_signal(barrier, inc=1, device_id=at_gy(k), device_id_type=MESH)
        return 0

    lax.fori_loop(1, n_gx, greet_x, 0)
    lax.fori_loop(1, n_gy, greet_y, 0)
    for side_x, side_y in SIDES:
        if side_x * side_y:
            corner = {"gx": at_gx(side_x)["gx"], "gy": at_gy(side_y)["gy"]}
            pl.semaphore_signal(barrier, inc=1, device_id=corner, device_id_type=MESH)

    def gx_copy(src, dst, send, recv, k, sign):
        return pltpu.make_async_remote_copy(
            src_ref=src,
            dst_ref=dst,
            send_sem=send,
            recv_sem=recv,
            device_id=at_gx(sign * k),
            device_id_type=MESH,
        )

    def gy_copy(src, dst, send, recv, k, sign):
        return pltpu.make_async_remote_copy(
            src_ref=src,
            dst_ref=dst,
            send_sem=send,
            recv_sem=recv,
            device_id=at_gy(sign * k),
            device_id_type=MESH,
        )

    def wait_for(ref, sem):
        pltpu.make_async_copy(ref, ref, sem).wait()

    def send_gx(src, dst, send, recv, sign):
        def body(k, _):
            gx_copy(src.at[k], dst.at[k], send, recv, k, sign).start()
            return 0

        lax.fori_loop(1, n_gx, body, 0)

    def inside(x, y):
        return (x >= 0) & (x < n_gx) & (y >= 0) & (y < n_gy)

    def rim_copies(f):
        span_x = {
            -1: (DEPTH, DEPTH + size_x, DEPTH),
            0: (DEPTH, DEPTH, size_x),
            1: (size_x, 0, DEPTH),
        }
        span_y = {
            -1: (EDGE, EDGE + size_y, PAD),
            0: (EDGE, EDGE, size_y),
            1: (EDGE + size_y - PAD, EDGE - PAD, PAD),
        }
        for i, (side_x, side_y) in enumerate(SIDES):
            def copy(i=i, side_x=side_x, side_y=side_y, x=span_x[side_x], y=span_y[side_y]):
                return pltpu.make_async_remote_copy(
                    src_ref=rim_part(f, x[0], x[2], y[0], y[2]),
                    dst_ref=rim_part(f, x[1], x[2], y[1], y[2]),
                    send_sem=rim_ss.at[f, i],
                    recv_sem=rim_rs.at[f, i],
                    device_id={"gx": at_gx(side_x)["gx"], "gy": at_gy(side_y)["gy"]},
                    device_id_type=MESH,
                )

            yield (
                inside(me_x + side_x, me_y + side_y),
                inside(me_x - side_x, me_y - side_y),
                copy,
            )

    def rim_part(f, x, count_x, y, count_y):
        return rim.at[pl.ds(f * planes + x, count_x), :, pl.ds(y, count_y), :]

    def rim_send(f, along_x=(True, False)):
        for (side_x, _), (sent, _, copy) in zip(SIDES, rim_copies(f)):
            if (side_x != 0) in along_x:
                pl.when(sent)(lambda: copy().start())

    def rim_wait(f, along_x=(True, False)):
        for (side_x, _), (_, received, copy) in zip(SIDES, rim_copies(f)):
            if (side_x != 0) in along_x:
                pl.when(received)(lambda: copy().wait_recv())

    def rim_wait_sent(f):
        for sent, _, copy in rim_copies(f):
            pl.when(sent)(lambda: copy().wait_send())

    def place(x, _):
        for h in range(2):
            rim[DEPTH + x, h, EDGE : EDGE + size_y, :] = beta[x, :, h * LANES : (h + 1) * LANES]
        return 0

    lax.fori_loop(0, size_x, place, 0)

    shift_gy = n_gy.bit_length() - 1
    own = owner[...]
    target[...] = ((own & (n_gy - 1)) - me_y & (n_gy - 1)) * n_gx + (
        (own >> shift_gy) - me_x & (n_gx - 1)
    )
    iota_t = lax.broadcasted_iota(jnp.int32, (owners, LANES), 0)
    iota_l = lax.broadcasted_iota(jnp.int32, (LANES, LANES), 0)
    above = lax.broadcasted_iota(jnp.int32, (LANES, 2 * LANES), 1)
    below = lax.broadcasted_iota(jnp.int32, (LANES, 2 * LANES), 0)
    counter = ((below < above) | (above >= LANES)).astype(BF16)
    offset = jnp.zeros((owners, LANES), F32)
    for j in range(rows):
        hit = target[j : j + 1, :] == iota_t
        hit_f = jnp.where(hit, 1.0, 0.0)
        hit_b = hit_f.astype(BF16)
        t_one[:, j * LANES : (j + 1) * LANES] = hit_b
        both = nn_dot(hit_b, counter)
        rank = jnp.sum(hit_f * (both[:, :LANES] + offset), axis=0, keepdims=True)
        offset = offset + both[:, LANES:]
        lane_of = rank.astype(jnp.int32) + me_y * cap
        l_one[:, j * LANES : (j + 1) * LANES] = jnp.where(lane_of == iota_l, 1.0, 0.0).astype(BF16)

    def to_rows(parts_of):
        stack = columns // owners
        parts = 0
        sizes = []
        for vector, split in parts_of:
            for j in range(rows):
                at = slice(j * LANES, (j + 1) * LANES)
                rows_j = split(vector[j : j + 1, :])
                for q, part in enumerate(rows_j):
                    tall, wide = (parts + q) % stack, (parts + q) // stack
                    c_one[
                        tall * owners : (tall + 1) * owners,
                        wide * points + j * LANES : wide * points + (j + 1) * LANES,
                    ] = t_one[:, at] * part
            sizes.append(len(rows_j))
            parts += len(rows_j)
        found = []
        for wide in range(-(-parts // stack)):
            tall = min(stack, parts - wide * stack) * owners
            sums = nt_dot(c_one[:tall, wide * points : (wide + 1) * points], l_one[...])
            found += [sums[q : q + owners, :] for q in range(0, tall, owners)]
        out = []
        for size in sizes:
            out.append(functools.reduce(lambda p, q: p + q, found[:size]))
            found = found[size:]
        return out

    def split_index(row):
        low = (row & (2 * LANES - 1)) + 1
        middle = (row >> 8) & (2 * LANES - 1)
        high = row >> 16
        return [
            x.astype(F32).astype(BF16) for x in (low, middle * 256, high * 65536)
        ]

    def forward_a(fields):
        for k in range(n_gy):
            for i, field in enumerate(fields):
                fa_send[k, i * n_gx : (i + 1) * n_gx, :] = field[k * n_gx : (k + 1) * n_gx, :]
        for k in range(1, n_gy):
            gy_copy(fa_send.at[k], fa_recv.at[k], a_ss.at[0], a_rs.at[0], k, 1).start()

    def forward_b():
        wait_for(fa_recv.at[pl.ds(1, n_gy - 1)], a_rs.at[0])
        both = fa_send[0]
        for k in range(1, n_gy):
            both = both + fa_recv[k]
        for k in range(n_gx):
            for i in range(4):
                fb_send[k, i : i + 1, :] = both[i * n_gx + k : i * n_gx + k + 1, :]
        send_gx(fb_send, fb_recv, b_ss.at[0], b_rs.at[0], 1)
        fb_recv[0] = fb_send[0]

    def forward_c():
        wait_for(fb_recv.at[pl.ds(1, n_gx - 1)], b_rs.at[0])
        return [fb_recv[:, i, :] for i in range(4)]

    def back_a(first, second, sums):
        for k in range(n_gx):
            rb_send[k, 0:1, :] = first[k : k + 1, :]
            rb_send[k, 1:2, :] = second[k : k + 1, :]
            rb_send[k, 2:3, :] = sums
            rb_send[k, 3:4, :] = sums
        send_gx(rb_send, rb_recv, b_ss.at[1], b_rs.at[1], -1)
        rb_recv[0] = rb_send[0]

    def back_b():
        wait_for(rb_recv.at[pl.ds(1, n_gx - 1)], b_rs.at[1])
        ra_send[0:n_gx, :] = rb_recv[:, 0, :]
        ra_send[n_gx : 2 * n_gx, :] = rb_recv[:, 1, :]
        sums = jnp.sum(rb_recv[:, 2, :], axis=0, keepdims=True)
        ra_send[2 * n_gx : 2 * n_gx + PAD, :] = jnp.broadcast_to(sums, (PAD, LANES))
        for k in range(1, n_gy):
            gy_copy(ra_send, ra_recv.at[k], a_ss.at[1], a_rs.at[1], k, -1).start()

    def back_c():
        wait_for(ra_recv.at[pl.ds(1, n_gy - 1)], a_rs.at[1])
        blocks = [ra_send[...]] + [ra_recv[k] for k in range(1, n_gy)]
        sums = blocks[0][2 * n_gx : 2 * n_gx + 1, :]
        for b in blocks[1:]:
            sums = sums + b[2 * n_gx : 2 * n_gx + 1, :]
        high, low = halves(
            jnp.concatenate(
                [b[i * n_gx : (i + 1) * n_gx, :] for i in range(2) for b in blocks], axis=0
            )
        )
        for j in range(rows):
            cols = slice(j * LANES, (j + 1) * LANES)
            lanes = l_one[:, cols]
            found = nn_dot(high, lanes) + nn_dot(low, lanes)
            hits = t_one[:, cols].astype(F32)
            for i in range(2):
                sampled[i, j : j + 1, :] = jnp.sum(
                    found[i * owners : (i + 1) * owners, :] * hits, axis=0, keepdims=True
                )
        return sampled[0], sampled[1], sums

    def sum_a(partial):
        pb_send[...] = jnp.broadcast_to(partial, pb_send.shape)

        def body(k, _):
            gx_copy(pb_send, pb_recv.at[k], p_ss.at[0], p_rs.at[0], k, 1).start()
            return 0

        lax.fori_loop(1, n_gx, body, 0)
        pb_recv[0] = pb_send[...]

    def sum_b():
        wait_for(pb_recv.at[pl.ds(1, n_gx - 1)], p_rs.at[0])
        pa_send[...] = jnp.sum(pb_recv[...], axis=0)
        for k in range(1, n_gy):
            gy_copy(pa_send, pa_recv.at[k], p_ss.at[1], p_rs.at[1], k, 1).start()
        pa_recv[0] = pa_send[...]

    def sum_c():
        wait_for(pa_recv.at[pl.ds(1, n_gy - 1)], p_rs.at[1])
        return jnp.sum(pa_recv[...], axis=0)[0:1, :]

    live = lax.broadcasted_iota(jnp.int32, (rows, LANES), 0) < count[...]
    rhs = jnp.where(live, jump[...], 0.0)
    steady = stiff[...]
    sw = jnp.where(live, weight[...], 0.0)
    fields = to_rows([(cell[...], split_index)] + [(x, halves) for x in (rhs, steady, sw)])
    pl.semaphore_wait(barrier, n_gx + n_gy + 2)
    forward_a(fields)
    rim_send(0)

    def rows_at(ref, x, h, start, n):
        return ref[x, h, pl.ds(start, n), :]

    def z_sides(low, high, lane):
        low_up, high_up = pltpu.roll(low, 1, 1), pltpu.roll(high, 1, 1)
        low_dn, high_dn = pltpu.roll(low, LANES - 1, 1), pltpu.roll(high, LANES - 1, 1)
        return (
            (low_up, jnp.where(lane == 0, low_up, high_up)),
            (jnp.where(lane == LANES - 1, high_dn, low_dn), high_dn),
        )

    def harmonic(a, b):
        both = a + b
        return 2.0 * a * b / jnp.where(both > 0, both, 1.0)

    def coefficients(x, y):
        row = y + PAD
        centre = [rows_at(rim, x + 1, h, row, PAD) for h in range(2)]
        before, after = z_sides(centre[0], centre[1], lane8)
        for h in range(2):
            c = centre[h]
            kxl = harmonic(c, rows_at(rim, x, h, row, PAD))
            kxh = harmonic(c, rows_at(rim, x + 2, h, row, PAD))
            kyl = harmonic(c, rows_at(rim, x + 1, h, row - 1, PAD))
            kyh = harmonic(c, rows_at(rim, x + 1, h, row + 1, PAD))
            kzl = harmonic(c, before[h])
            kzh = harmonic(c, after[h])
            if h == 0:
                kzl = jnp.where(lane8 == 0, 0.0, kzl)
            else:
                kzh = jnp.where(lane8 == LANES - 1, 0.0, kzh)
            inverse = 1.0 / (SHIFT + kxl + kxh + kyl + kyh + kzl + kzh)
            at = (x, h, pl.ds(y, PAD), slice(None))
            invd[at] = inverse
            axl[at] = kxl * inverse
            axh[at] = kxh * inverse
            ayl[at] = kyl * inverse
            ayh[at] = kyh * inverse
            azl[at] = kzl * inverse
            azh[at] = kzh * inverse

    ends = planes - 2 - DEPTH

    def inner_planes(rows_of):
        def body(i, _):
            for x in range(2):
                for y in rows_of:
                    coefficients(DEPTH + 2 * i + x, y)
            return 0

        lax.fori_loop(0, (ends - DEPTH) // 2, body, 0)

    def end_planes(i, _):
        for x in (i, ends + i):
            for y in range(0, size_y + 2 * PAD, PAD):
                coefficients(x, y)
        return 0

    inner_planes(range(2 * PAD, size_y, PAD))
    forward_b()
    rim_wait(0, (False,))
    inner_planes((0, PAD, size_y, size_y + PAD))
    rim_wait(0, (True,))
    lax.fori_loop(0, DEPTH, end_planes, 0)

    index, slot_rhs, slot_steady, slot_sw = forward_c()
    index = index.astype(jnp.int32) - 1
    z_at[...] = jnp.where(index < 0, -1, index & (size_z - 1))
    slot_val[...] = index >> 8
    near = list(range(DEPTH)) + list(range(size_x - DEPTH, size_x))
    middle = range(DEPTH, size_x - DEPTH)
    runs = [
        [(x, 0, size_y) for x in near[:DEPTH]],
        [(x, 0, size_y) for x in near[DEPTH:]],
        [(x, y, PAD) for x in middle for y in (0, size_y - PAD)],
        [(x, PAD, size_y - 2 * PAD) for x in middle],
    ]
    iota_c = jnp.concatenate(
        [
            lax.broadcasted_iota(jnp.int32, (n, LANES), 0) + (x * size_y + y)
            for group in runs
            for x, y, n in group
        ],
        axis=0,
    )
    per = chunk // LANES
    iota_z = lax.broadcasted_iota(jnp.int32, (size_z, LANES), 0)
    for j in range(n_gx):
        row = slot_val[j : j + 1, :]
        c_one[:, j * LANES : (j + 1) * LANES] = jnp.where(row == iota_c, 1.0, 0.0).astype(BF16)

    def spread_grid(f, values):
        picked[...] = values
        for j in range(n_gx):
            row = picked[j : j + 1, :]
            hit = z_at[j : j + 1, :] == iota_z
            high = row.astype(BF16).astype(F32)
            cols = slice(j * LANES, (j + 1) * LANES)
            z_both[:size_z, cols] = jnp.where(hit, high, 0.0).astype(BF16)
            z_both[size_z:, cols] = jnp.where(hit, row - high, 0.0).astype(BF16)
        at = 0
        for i, group in enumerate(runs):
            count = sum(n for _, _, n in group)
            found = nt_dot(c_one[at : at + count, :], z_both[...])
            source = found[:, :size_z] + found[:, size_z:]
            at += count
            row = 0
            for x, y, n in group:
                for h in range(2):
                    rim[f * planes + DEPTH + x, h, EDGE + y : EDGE + y + n, :] = (
                        source[row : row + n, h * LANES : (h + 1) * LANES]
                        * invd[DEPTH - 1 + x, h, PAD + y : PAD + y + n, :]
                    )
                row += n
            if i == 1:
                rim_send(f, (True,))
            if i == 2:
                rim_send(f, (False,))

    def sample_grid(p):
        at = 0
        for group in runs:
            for x, y, n in group:
                for h in range(2):
                    field_c[at : at + n, h * LANES : (h + 1) * LANES] = u[
                        p, DEPTH + x, h, EDGE + y : EDGE + y + n, :
                    ]
                at += n
        for i in range(columns // LANES):
            cols = slice(i * LANES, (i + 1) * LANES)
            for h in range(2):
                high, low = halves(field_c[cols, h * LANES : (h + 1) * LANES].T)
                field_t[h * LANES : (h + 1) * LANES, cols] = high
                field_t[size_z + h * LANES : size_z + (h + 1) * LANES, cols] = low

        def body(i, _):
            found = nn_dot(
                field_t[...], c_one[:, pl.ds(pl.multiple_of(i * chunk, LANES), chunk)]
            )
            for q in range(per):
                j = i * per + q
                hit = z_at[pl.ds(j, 1), :] == iota_z
                cols = slice(q * LANES, (q + 1) * LANES)
                both = found[:size_z, cols] + found[size_z:, cols]
                picked[pl.ds(j, 1), :] = jnp.sum(
                    jnp.where(hit, both, 0.0), axis=0, keepdims=True
                )
            return 0

        lax.fori_loop(0, slots // chunk, body, 0)

    def relax(f, step, x, y, n, first, second):
        lane = lax.broadcasted_iota(jnp.int32, (n, LANES), 1)
        row = y + PAD

        def field(x, h, row):
            if step == 0:
                return rim[f * planes + x, h, pl.ds(row, n), :]
            return u[(step - 1) % 2, x, h, pl.ds(row, n), :]

        centre = [field(x, h, row) for h in range(2)]
        before, after = z_sides(centre[0], centre[1], lane)
        for h in range(2):
            at = (x - 1, h, pl.ds(y, n), slice(None))
            sides = axl[at] * field(x - 1, h, row) + axh[at] * field(x + 1, h, row)
            sides += ayl[at] * field(x, h, row - 1) + ayh[at] * field(x, h, row + 1)
            sides += azl[at] * before[h] + azh[at] * after[h]
            if step == 0:
                now = centre[h] * (1.0 / THETA)
                update = first * now + second * (centre[h] + (sides - centre[h]) * (1.0 / THETA))
            else:
                now = centre[h]
                update = first * d[at] + second * (rim[f * planes + x, h, pl.ds(row, n), :] + sides - now)
            d[at] = update
            u[step % 2, x, h, pl.ds(row, n), :] = now + update

    def pressure(f):
        rim_wait(f, (False,))
        factors = sweep_factors()

        def step_planes(step, start, count):
            low, high = (0, size_y + 2 * PAD) if step < CHEB - 2 else (PAD, size_y + PAD)
            n = (high - low) // 2
            for x in range(count):
                for y in (low, low + n):
                    relax(f, step, start + x, y, n, *factors[step])

        for step in range(CHEB - 1):
            step_planes(step, DEPTH + step + 1, size_x - 2 * (step + 1))
        rim_wait(f, (True,))
        for step in range(CHEB - 1):

            def body(side, _):
                step_planes(step, step + 1 + side * (planes - DEPTH - 2 * (step + 1)), DEPTH)
                return 0

            lax.fori_loop(0, 2, body, 0)
        return (CHEB - 2) % 2

    spread_grid(1, slot_sw * slot_rhs)
    sample_grid(pressure(1))
    got_1 = picked[...]
    slot_a = slot_steady * slot_rhs + slot_sw * got_1
    sum_a(pack_row([total(slot_rhs * slot_rhs), total(slot_rhs * slot_a)]))
    spread_grid(2, slot_sw * slot_a)
    sum_b()
    end = pressure(2)
    sum_bb, sum_ab = unpack_row(sum_c(), 2)
    sample_grid(end)
    got_2 = picked[...]
    start = jnp.sqrt(sum_bb + EPS)
    scale = 1.0 / start
    h_11 = sum_ab * scale * scale

    def basis(first, image, image_of_image):
        v_1 = first * scale
        w_1 = image * scale
        return v_1, w_1, w_1 - h_11 * v_1, image_of_image * scale - h_11 * w_1

    v_1, _, z, s_z = basis(slot_rhs, slot_a, slot_steady * slot_a + slot_sw * got_2)
    pairs = ((z, z), (s_z, v_1), (s_z, z), (s_z, s_z), (v_1, v_1), (v_1, z))
    back_a(got_1, got_2, pack_row([total(p * q) for p, q in pairs]))
    back_b()
    got_1, got_2, sums = back_c()
    image_1 = steady * rhs + sw * got_1
    v_1, w_1, z, s_z = basis(rhs, image_1, jnp.where(live, steady, 0.0) * image_1 + sw * got_2)
    zz, szv, szz, szsz, v1v1, v1z = unpack_row(sums, 6)
    h_21 = jnp.sqrt(zz + EPS)
    inverse = 1.0 / h_21
    v_2 = z * inverse
    w_2 = s_z * inverse
    w2v1, w2v2, w2w2 = szv * inverse, szz * inverse * inverse, szsz * inverse * inverse
    v1v2, v2v2 = v1z * inverse, zz * inverse * inverse
    h_12 = w2v1
    h_22 = w2v2 - h_12 * v1v2
    square = (
        w2w2
        + h_12 * h_12 * v1v1
        + h_22 * h_22 * v2v2
        - 2.0 * h_12 * w2v1
        - 2.0 * h_22 * w2v2
        + 2.0 * h_12 * h_22 * v1v2
    )
    h_32 = jnp.sqrt(jnp.maximum(square, 0.0) + EPS)
    y_1, y_2 = least_squares(start, [[h_11, h_21], [h_12, h_22, h_32]])
    sol[...] = y_1 * v_1 + y_2 * v_2
    res[...] = rhs - y_1 * w_1 - y_2 * w_2

    for f in range(3):
        rim_wait_sent(f)
    wait_for(fa_send.at[pl.ds(1, n_gy - 1)], a_ss.at[0])
    wait_for(ra_recv.at[pl.ds(1, n_gy - 1)], a_ss.at[1])
    wait_for(fb_send.at[pl.ds(1, n_gx - 1)], b_ss.at[0])
    wait_for(rb_send.at[pl.ds(1, n_gx - 1)], b_ss.at[1])
    wait_for(pb_recv.at[pl.ds(1, n_gx - 1)], p_ss.at[0])
    wait_for(pa_recv.at[pl.ds(1, n_gy - 1)], p_ss.at[1])


def on_device(n_gx, n_gy, beta, jump, stiff, weight, owner, cell, count):
    size_x, size_y, size_z = beta.shape
    points = jump.shape[0]
    rows = points // LANES
    owners = n_gx * n_gy
    columns = size_x * size_y
    planes = size_x + 2 * DEPTH
    wide = (planes, 2, size_y + 4 * PAD, LANES)
    tile = (planes - 2, 2, size_y + 2 * PAD, LANES)
    slots = n_gx * LANES
    dma = pltpu.SemaphoreType.DMA
    scratch = [
        pltpu.VMEM((owners, points), BF16),
        pltpu.VMEM((LANES, points), BF16),
        pltpu.VMEM((rows, LANES), jnp.int32),
        pltpu.VMEM((rows, LANES), jnp.int32),
        pltpu.VMEM((3 * planes,) + wide[1:], F32),
        pltpu.VMEM((2,) + wide, F32),
        pltpu.VMEM(tile, F32),
        pltpu.VMEM(tile, F32),
        pltpu.VMEM(tile, F32),
        pltpu.VMEM(tile, F32),
        pltpu.VMEM(tile, F32),
        pltpu.VMEM(tile, F32),
        pltpu.VMEM(tile, F32),
        pltpu.VMEM(tile, F32),
        pltpu.VMEM((columns, size_z), F32),
        pltpu.VMEM((2 * size_z, columns), BF16),
        pltpu.VMEM((columns, slots), BF16),
        pltpu.VMEM((2 * size_z, slots), BF16),
        pltpu.VMEM((n_gx, LANES), jnp.int32),
        pltpu.VMEM((n_gx, LANES), jnp.int32),
        pltpu.VMEM((n_gx, LANES), F32),
        pltpu.VMEM((2, rows, LANES), F32),
        pltpu.VMEM((n_gy, 4 * n_gx, LANES), F32),
        pltpu.VMEM((n_gy, 4 * n_gx, LANES), F32),
        pltpu.VMEM((n_gx, 4, LANES), F32),
        pltpu.VMEM((n_gx, 4, LANES), F32),
        pltpu.VMEM((n_gx, 4, LANES), F32),
        pltpu.VMEM((n_gx, 4, LANES), F32),
        pltpu.VMEM((2 * n_gx + PAD, LANES), F32),
        pltpu.VMEM((n_gy, 2 * n_gx + PAD, LANES), F32),
        pltpu.VMEM((2, LANES), F32),
        pltpu.VMEM((n_gx, 2, LANES), F32),
        pltpu.VMEM((2, LANES), F32),
        pltpu.VMEM((n_gy, 2, LANES), F32),
    ] + [dma((2,))] * 6 + [dma((3, len(SIDES)))] * 2
    vmem = pl.BlockSpec(memory_space=pltpu.VMEM)
    out = jax.ShapeDtypeStruct((rows, LANES), F32)
    solution, residual = pl.pallas_call(
        functools.partial(kernel, n_gx, n_gy),
        out_shape=(out, out),
        in_specs=[vmem] * 7,
        out_specs=(vmem, vmem),
        scratch_shapes=scratch,
        compiler_params=pltpu.CompilerParams(
            collective_id=0, has_side_effects=True, vmem_limit_bytes=56 * 1024 * 1024
        ),
    )(
        beta,
        jump.reshape(rows, LANES),
        stiff.reshape(rows, LANES),
        weight.reshape(rows, LANES),
        owner.reshape(rows, LANES),
        cell.reshape(rows, LANES),
        count.reshape(1, 1),
    )
    return solution.reshape(points), residual.reshape(points)


def solution(mesh):
    points = P(("gx", "gy"))
    return jax.shard_map(
        functools.partial(on_device, mesh.shape["gx"], mesh.shape["gy"]),
        mesh=mesh,
        in_specs=(P("gx", "gy", None), points, points, points, P(("gx", "gy"), None), points, points),
        out_specs=(points, points),
        check_vma=False,
    )
```

```python
import functools

import jax
import jax.numpy as jnp
from jax import lax
from jax.experimental import pallas as pl
from jax.experimental.pallas import tpu as pltpu
from jax.sharding import PartitionSpec as P

CHEB = 6
SHIFT = 0.01
THETA = 1.025
DELTA = 0.975
SIGMA = THETA / DELTA
EPS = 1e-06
LANES = 128
PAD = 8
EDGE = 2 * PAD
DEPTH = CHEB - 1
SIDES = [(x, y) for x in (-1, 0, 1) for y in (-1, 0, 1) if (x, y) != (0, 0)]
MESH = pl.DeviceIdType.MESH
F32 = jnp.float32
BF16 = jnp.bfloat16
CHUNK = 1024


def sweep_factors():
    factors = []
    ratio = 1.0 / SIGMA
    for _ in range(CHEB - 1):
        ratio_next = 1.0 / (2.0 * SIGMA - ratio)
        factors.append((ratio_next * ratio, 2.0 * ratio_next / DELTA))
        ratio = ratio_next
    return factors


def least_squares(start, columns):
    count = len(columns)
    targets = [start] + [start * 0.0 for unused in range(count)]
    cosines = []
    sines = []
    upper = []
    for outer in range(count):
        column = list(columns[outer])
        for inner in range(outer):
            first = cosines[inner] * column[inner] + sines[inner] * column[inner + 1]
            second = -sines[inner] * column[inner] + cosines[inner] * column[inner + 1]
            column[inner] = first
            column[inner + 1] = second
        radius = jnp.sqrt(column[outer] * column[outer] + column[outer + 1] * column[outer + 1])
        cosine = column[outer] / radius
        sine = column[outer + 1] / radius
        column[outer] = radius
        targets[outer + 1] = -sine * targets[outer]
        targets[outer] = cosine * targets[outer]
        cosines.append(cosine)
        sines.append(sine)
        upper.append(column)
    coeffs = [None] * count
    for outer in reversed(range(count)):
        total = targets[outer]
        for later in range(outer + 1, count):
            total = total - upper[later][outer] * coeffs[later]
        coeffs[outer] = total / upper[outer][outer]
    return coeffs


def halves(x):
    high = x.astype(BF16)
    low = (x - high.astype(F32)).astype(BF16)
    return high, low


def nt_dot(a, b):
    return lax.dot_general(a, b, (((1,), (1,)), ((), ())), preferred_element_type=F32)


def nn_dot(a, b):
    return lax.dot_general(a, b, (((1,), (0,)), ((), ())), preferred_element_type=F32)


def total(x):
    return jnp.sum(jnp.sum(x, axis=0, keepdims=True), axis=1, keepdims=True)


def pack_row(values):
    lane = lax.broadcasted_iota(jnp.int32, (1, LANES), 1)
    row = jnp.zeros((1, LANES), F32)
    for at, value in enumerate(values):
        row = jnp.where(lane == at, value, row)
    return row


def unpack_row(row, count):
    lane = lax.broadcasted_iota(jnp.int32, (1, LANES), 1)
    return [
        jnp.sum(jnp.where(lane == at, row, 0.0), axis=1, keepdims=True) for at in range(count)
    ]


def kernel(
    n_gx,
    n_gy,
    beta,
    jump,
    stiff,
    weight,
    owner,
    cell,
    count,
    sol,
    res,
    t_one,
    l_one,
    target,
    lanes_at,
    rim,
    u,
    d,
    invd,
    axl,
    axh,
    ayl,
    ayh,
    azl,
    azh,
    field_c,
    field_t,
    c_one,
    z_both,
    z_at,
    slot_val,
    picked,
    sampled,
    fa_send,
    fa_recv,
    fb_send,
    fb_recv,
    rb_send,
    rb_recv,
    ra_send,
    ra_recv,
    pb_send,
    pb_recv,
    pa_send,
    pa_recv,
    a_ss,
    a_rs,
    b_ss,
    b_rs,
    p_ss,
    p_rs,
    rim_ss,
    rim_rs,
):
    me_x = lax.axis_index("gx")
    me_y = lax.axis_index("gy")
    size_x, size_y, size_z = beta.shape
    rows = jump.shape[0]
    points = rows * LANES
    owners = n_gx * n_gy
    cap = LANES // n_gy
    slots = n_gx * LANES
    columns = size_x * size_y
    chunk = min(CHUNK, slots)
    lane8 = lax.broadcasted_iota(jnp.int32, (PAD, LANES), 1)

    def at_gx(shift):
        return {"gx": lax.rem(me_x + shift + n_gx, n_gx), "gy": me_y}

    def at_gy(shift):
        return {"gx": me_x, "gy": lax.rem(me_y + shift + n_gy, n_gy)}

    planes = size_x + 2 * DEPTH

    def clear_planes(first):
        for f in range(3):
            for x in range(DEPTH):
                at = f * planes + first + x
                rim[at] = jnp.zeros(rim.shape[1:], F32)

    def clear_rows(first):
        def body(x, _):
            rim[x, :, first : first + EDGE, :] = jnp.zeros((2, EDGE, LANES), F32)
            return 0

        lax.fori_loop(0, rim.shape[0], body, 0)

    pl.when(me_x == 0)(lambda: clear_planes(0))
    pl.when(me_x == n_gx - 1)(lambda: clear_planes(size_x + DEPTH))
    pl.when(me_y == 0)(lambda: clear_rows(0))
    pl.when(me_y == n_gy - 1)(lambda: clear_rows(EDGE + size_y))

    barrier = pltpu.get_barrier_semaphore()

    def greet_x(k, _):
        pl.semaphore_signal(barrier, inc=1, device_id=at_gx(k), device_id_type=MESH)
        return 0

    def greet_y(k, _):
        pl.semaphore_signal(barrier, inc=1, device_id=at_gy(k), device_id_type=MESH)
        return 0

    lax.fori_loop(1, n_gx, greet_x, 0)
    lax.fori_loop(1, n_gy, greet_y, 0)
    for side_x, side_y in SIDES:
        if side_x * side_y:
            corner = {"gx": at_gx(side_x)["gx"], "gy": at_gy(side_y)["gy"]}
            pl.semaphore_signal(barrier, inc=1, device_id=corner, device_id_type=MESH)

    def gx_copy(src, dst, send, recv, k, sign):
        return pltpu.make_async_remote_copy(
            src_ref=src,
            dst_ref=dst,
            send_sem=send,
            recv_sem=recv,
            device_id=at_gx(sign * k),
            device_id_type=MESH,
        )

    def gy_copy(src, dst, send, recv, k, sign):
        return pltpu.make_async_remote_copy(
            src_ref=src,
            dst_ref=dst,
            send_sem=send,
            recv_sem=recv,
            device_id=at_gy(sign * k),
            device_id_type=MESH,
        )

    def wait_for(ref, sem):
        pltpu.make_async_copy(ref, ref, sem).wait()

    def send_gx(src, dst, send, recv, sign):
        def body(k, _):
            gx_copy(src.at[k], dst.at[k], send, recv, k, sign).start()
            return 0

        lax.fori_loop(1, n_gx, body, 0)

    def inside(x, y):
        return (x >= 0) & (x < n_gx) & (y >= 0) & (y < n_gy)

    def rim_copies(f):
        span_x = {
            -1: (DEPTH, DEPTH + size_x, DEPTH),
            0: (DEPTH, DEPTH, size_x),
            1: (size_x, 0, DEPTH),
        }
        span_y = {
            -1: (EDGE, EDGE + size_y, PAD),
            0: (EDGE, EDGE, size_y),
            1: (EDGE + size_y - PAD, EDGE - PAD, PAD),
        }
        for i, (side_x, side_y) in enumerate(SIDES):
            def copy(i=i, side_x=side_x, side_y=side_y, x=span_x[side_x], y=span_y[side_y]):
                return pltpu.make_async_remote_copy(
                    src_ref=rim_part(f, x[0], x[2], y[0], y[2]),
                    dst_ref=rim_part(f, x[1], x[2], y[1], y[2]),
                    send_sem=rim_ss.at[f, i],
                    recv_sem=rim_rs.at[f, i],
                    device_id={"gx": at_gx(side_x)["gx"], "gy": at_gy(side_y)["gy"]},
                    device_id_type=MESH,
                )

            yield (
                inside(me_x + side_x, me_y + side_y),
                inside(me_x - side_x, me_y - side_y),
                copy,
            )

    def rim_part(f, x, count_x, y, count_y):
        return rim.at[pl.ds(f * planes + x, count_x), :, pl.ds(y, count_y), :]

    def rim_send(f, along_x=(True, False)):
        for (side_x, _), (sent, _, copy) in zip(SIDES, rim_copies(f)):
            if (side_x != 0) in along_x:
                pl.when(sent)(lambda: copy().start())

    def rim_wait(f, along_x=(True, False)):
        for (side_x, _), (_, received, copy) in zip(SIDES, rim_copies(f)):
            if (side_x != 0) in along_x:
                pl.when(received)(lambda: copy().wait_recv())

    def rim_wait_sent(f):
        for sent, _, copy in rim_copies(f):
            pl.when(sent)(lambda: copy().wait_send())

    def place(x, _):
        for h in range(2):
            rim[DEPTH + x, h, EDGE : EDGE + size_y, :] = beta[x, :, h * LANES : (h + 1) * LANES]
        return 0

    lax.fori_loop(0, size_x, place, 0)

    shift_gy = n_gy.bit_length() - 1
    own = owner[...]
    target[...] = ((own & (n_gy - 1)) - me_y & (n_gy - 1)) * n_gx + (
        (own >> shift_gy) - me_x & (n_gx - 1)
    )
    iota_t = lax.broadcasted_iota(jnp.int32, (owners, LANES), 0)
    iota_l = lax.broadcasted_iota(jnp.int32, (LANES, LANES), 0)
    above = lax.broadcasted_iota(jnp.int32, (LANES, 2 * LANES), 1)
    below = lax.broadcasted_iota(jnp.int32, (LANES, 2 * LANES), 0)
    counter = ((below < above) | (above >= LANES)).astype(BF16)
    offset = jnp.zeros((owners, LANES), F32)
    for j in range(rows):
        hit = target[j : j + 1, :] == iota_t
        hit_f = jnp.where(hit, 1.0, 0.0)
        hit_b = hit_f.astype(BF16)
        t_one[:, j * LANES : (j + 1) * LANES] = hit_b
        both = nn_dot(hit_b, counter)
        rank = jnp.sum(hit_f * (both[:, :LANES] + offset), axis=0, keepdims=True)
        offset = offset + both[:, LANES:]
        lane_of = rank.astype(jnp.int32) + me_y * cap
        l_one[:, j * LANES : (j + 1) * LANES] = jnp.where(lane_of == iota_l, 1.0, 0.0).astype(BF16)

    def to_rows(parts_of):
        stack = columns // owners
        parts = 0
        sizes = []
        for vector, split in parts_of:
            for j in range(rows):
                at = slice(j * LANES, (j + 1) * LANES)
                rows_j = split(vector[j : j + 1, :])
                for q, part in enumerate(rows_j):
                    tall, wide = (parts + q) % stack, (parts + q) // stack
                    c_one[
                        tall * owners : (tall + 1) * owners,
                        wide * points + j * LANES : wide * points + (j + 1) * LANES,
                    ] = t_one[:, at] * part
            sizes.append(len(rows_j))
            parts += len(rows_j)
        found = []
        for wide in range(-(-parts // stack)):
            tall = min(stack, parts - wide * stack) * owners
            sums = nt_dot(c_one[:tall, wide * points : (wide + 1) * points], l_one[...])
            found += [sums[q : q + owners, :] for q in range(0, tall, owners)]
        out = []
        for size in sizes:
            out.append(functools.reduce(lambda p, q: p + q, found[:size]))
            found = found[size:]
        return out

    def split_index(row):
        low = (row & (2 * LANES - 1)) + 1
        middle = (row >> 8) & (2 * LANES - 1)
        high = row >> 16
        return [
            x.astype(F32).astype(BF16) for x in (low, middle * 256, high * 65536)
        ]

    def forward_a(fields):
        for k in range(n_gy):
            for i, field in enumerate(fields):
                fa_send[k, i * n_gx : (i + 1) * n_gx, :] = field[k * n_gx : (k + 1) * n_gx, :]
        for k in range(1, n_gy):
            gy_copy(fa_send.at[k], fa_recv.at[k], a_ss.at[0], a_rs.at[0], k, 1).start()

    def forward_b():
        wait_for(fa_recv.at[pl.ds(1, n_gy - 1)], a_rs.at[0])
        both = fa_send[0]
        for k in range(1, n_gy):
            both = both + fa_recv[k]
        for k in range(n_gx):
            for i in range(4):
                fb_send[k, i : i + 1, :] = both[i * n_gx + k : i * n_gx + k + 1, :]
        send_gx(fb_send, fb_recv, b_ss.at[0], b_rs.at[0], 1)
        fb_recv[0] = fb_send[0]

    def forward_c():
        wait_for(fb_recv.at[pl.ds(1, n_gx - 1)], b_rs.at[0])
        return [fb_recv[:, i, :] for i in range(4)]

    def back_a(first, second, sums):
        for k in range(n_gx):
            rb_send[k, 0:1, :] = first[k : k + 1, :]
            rb_send[k, 1:2, :] = second[k : k + 1, :]
            rb_send[k, 2:3, :] = sums
            rb_send[k, 3:4, :] = sums
        send_gx(rb_send, rb_recv, b_ss.at[1], b_rs.at[1], -1)
        rb_recv[0] = rb_send[0]

    def back_b():
        wait_for(rb_recv.at[pl.ds(1, n_gx - 1)], b_rs.at[1])
        ra_send[0:n_gx, :] = rb_recv[:, 0, :]
        ra_send[n_gx : 2 * n_gx, :] = rb_recv[:, 1, :]
        sums = jnp.sum(rb_recv[:, 2, :], axis=0, keepdims=True)
        ra_send[2 * n_gx : 2 * n_gx + PAD, :] = jnp.broadcast_to(sums, (PAD, LANES))
        for k in range(1, n_gy):
            gy_copy(ra_send, ra_recv.at[k], a_ss.at[1], a_rs.at[1], k, -1).start()

    def back_c():
        wait_for(ra_recv.at[pl.ds(1, n_gy - 1)], a_rs.at[1])
        blocks = [ra_send[...]] + [ra_recv[k] for k in range(1, n_gy)]
        sums = blocks[0][2 * n_gx : 2 * n_gx + 1, :]
        for b in blocks[1:]:
            sums = sums + b[2 * n_gx : 2 * n_gx + 1, :]
        high, low = halves(
            jnp.concatenate(
                [b[i * n_gx : (i + 1) * n_gx, :] for i in range(2) for b in blocks], axis=0
            )
        )
        for j in range(rows):
            cols = slice(j * LANES, (j + 1) * LANES)
            lanes = l_one[:, cols]
            found = nn_dot(high, lanes) + nn_dot(low, lanes)
            hits = t_one[:, cols].astype(F32)
            for i in range(2):
                sampled[i, j : j + 1, :] = jnp.sum(
                    found[i * owners : (i + 1) * owners, :] * hits, axis=0, keepdims=True
                )
        return sampled[0], sampled[1], sums

    def sum_a(partial):
        pb_send[...] = jnp.broadcast_to(partial, pb_send.shape)

        def body(k, _):
            gx_copy(pb_send, pb_recv.at[k], p_ss.at[0], p_rs.at[0], k, 1).start()
            return 0

        lax.fori_loop(1, n_gx, body, 0)
        pb_recv[0] = pb_send[...]

    def sum_b():
        wait_for(pb_recv.at[pl.ds(1, n_gx - 1)], p_rs.at[0])
        pa_send[...] = jnp.sum(pb_recv[...], axis=0)
        for k in range(1, n_gy):
            gy_copy(pa_send, pa_recv.at[k], p_ss.at[1], p_rs.at[1], k, 1).start()
        pa_recv[0] = pa_send[...]

    def sum_c():
        wait_for(pa_recv.at[pl.ds(1, n_gy - 1)], p_rs.at[1])
        return jnp.sum(pa_recv[...], axis=0)[0:1, :]

    live = lax.broadcasted_iota(jnp.int32, (rows, LANES), 0) < count[...]
    rhs = jnp.where(live, jump[...], 0.0)
    steady = stiff[...]
    sw = jnp.where(live, weight[...], 0.0)
    fields = to_rows([(cell[...], split_index)] + [(x, halves) for x in (rhs, steady, sw)])
    pl.semaphore_wait(barrier, n_gx + n_gy + 2)
    forward_a(fields)
    rim_send(0)

    def rows_at(ref, x, h, start, n):
        return ref[x, h, pl.ds(start, n), :]

    def z_sides(low, high, lane):
        low_up, high_up = pltpu.roll(low, 1, 1), pltpu.roll(high, 1, 1)
        low_dn, high_dn = pltpu.roll(low, LANES - 1, 1), pltpu.roll(high, LANES - 1, 1)
        return (
            (low_up, jnp.where(lane == 0, low_up, high_up)),
            (jnp.where(lane == LANES - 1, high_dn, low_dn), high_dn),
        )

    def harmonic(a, b):
        both = a + b
        return 2.0 * a * b / jnp.where(both > 0, both, 1.0)

    def coefficients(x, y):
        row = y + PAD
        centre = [rows_at(rim, x + 1, h, row, PAD) for h in range(2)]
        before, after = z_sides(centre[0], centre[1], lane8)
        for h in range(2):
            c = centre[h]
            kxl = harmonic(c, rows_at(rim, x, h, row, PAD))
            kxh = harmonic(c, rows_at(rim, x + 2, h, row, PAD))
            kyl = harmonic(c, rows_at(rim, x + 1, h, row - 1, PAD))
            kyh = harmonic(c, rows_at(rim, x + 1, h, row + 1, PAD))
            kzl = harmonic(c, before[h])
            kzh = harmonic(c, after[h])
            if h == 0:
                kzl = jnp.where(lane8 == 0, 0.0, kzl)
            else:
                kzh = jnp.where(lane8 == LANES - 1, 0.0, kzh)
            inverse = 1.0 / (SHIFT + kxl + kxh + kyl + kyh + kzl + kzh)
            at = (x, h, pl.ds(y, PAD), slice(None))
            invd[at] = inverse
            axl[at] = kxl * inverse
            axh[at] = kxh * inverse
            ayl[at] = kyl * inverse
            ayh[at] = kyh * inverse
            azl[at] = kzl * inverse
            azh[at] = kzh * inverse

    ends = planes - 2 - DEPTH

    def inner_planes(rows_of):
        def body(i, _):
            for x in range(2):
                for y in rows_of:
                    coefficients(DEPTH + 2 * i + x, y)
            return 0

        lax.fori_loop(0, (ends - DEPTH) // 2, body, 0)

    def end_planes(i, _):
        for x in (i, ends + i):
            for y in range(0, size_y + 2 * PAD, PAD):
                coefficients(x, y)
        return 0

    inner_planes(range(2 * PAD, size_y, PAD))
    forward_b()
    rim_wait(0, (False,))
    inner_planes((0, PAD, size_y, size_y + PAD))
    rim_wait(0, (True,))
    lax.fori_loop(0, DEPTH, end_planes, 0)

    index, slot_rhs, slot_steady, slot_sw = forward_c()
    index = index.astype(jnp.int32) - 1
    z_at[...] = jnp.where(index < 0, -1, index & (size_z - 1))
    slot_val[...] = index >> 8
    near = list(range(DEPTH)) + list(range(size_x - DEPTH, size_x))
    middle = range(DEPTH, size_x - DEPTH)
    runs = [
        [(x, 0, size_y) for x in near[:DEPTH]],
        [(x, 0, size_y) for x in near[DEPTH:]],
        [(x, y, PAD) for x in middle for y in (0, size_y - PAD)],
        [(x, PAD, size_y - 2 * PAD) for x in middle],
    ]
    iota_c = jnp.concatenate(
        [
            lax.broadcasted_iota(jnp.int32, (n, LANES), 0) + (x * size_y + y)
            for group in runs
            for x, y, n in group
        ],
        axis=0,
    )
    per = chunk // LANES
    iota_16 = iota_c.astype(jnp.int16)
    iota_z = lax.broadcasted_iota(jnp.int32, (size_z, LANES), 0)
    for j in range(n_gx):
        row = slot_val[j : j + 1, :]
        c_one[:, j * LANES : (j + 1) * LANES] = jnp.where(
            row.astype(jnp.int16) == iota_16, jnp.ones((), BF16), jnp.zeros((), BF16)
        )

    def spread_grid(f, values):
        picked[...] = values
        for j in range(n_gx):
            row = picked[j : j + 1, :]
            hit = z_at[j : j + 1, :] == iota_z
            high = row.astype(BF16).astype(F32)
            cols = slice(j * LANES, (j + 1) * LANES)
            z_both[:size_z, cols] = jnp.where(hit, high, 0.0).astype(BF16)
            z_both[size_z:, cols] = jnp.where(hit, row - high, 0.0).astype(BF16)
        at = 0
        for i, group in enumerate(runs):
            count = sum(n for _, _, n in group)
            found = nt_dot(c_one[at : at + count, :], z_both[...])
            source = found[:, :size_z] + found[:, size_z:]
            at += count
            row = 0
            for x, y, n in group:
                for h in range(2):
                    rim[f * planes + DEPTH + x, h, EDGE + y : EDGE + y + n, :] = (
                        source[row : row + n, h * LANES : (h + 1) * LANES]
                        * invd[DEPTH - 1 + x, h, PAD + y : PAD + y + n, :]
                    )
                row += n
            if i == 1:
                rim_send(f, (True,))
            if i == 2:
                rim_send(f, (False,))

    def sample_grid(p):
        at = 0
        for group in runs:
            for x, y, n in group:
                for h in range(2):
                    field_c[at : at + n, h * LANES : (h + 1) * LANES] = u[
                        p, DEPTH + x, h, EDGE + y : EDGE + y + n, :
                    ]
                at += n
        for i in range(columns // LANES):
            cols = slice(i * LANES, (i + 1) * LANES)
            for h in range(2):
                high, low = halves(field_c[cols, h * LANES : (h + 1) * LANES].T)
                field_t[h * LANES : (h + 1) * LANES, cols] = high
                field_t[size_z + h * LANES : size_z + (h + 1) * LANES, cols] = low

        def body(i, _):
            found = nn_dot(
                field_t[...], c_one[:, pl.ds(pl.multiple_of(i * chunk, LANES), chunk)]
            )
            for q in range(per):
                j = i * per + q
                hit = z_at[pl.ds(j, 1), :] == iota_z
                cols = slice(q * LANES, (q + 1) * LANES)
                both = found[:size_z, cols] + found[size_z:, cols]
                picked[pl.ds(j, 1), :] = jnp.sum(
                    jnp.where(hit, both, 0.0), axis=0, keepdims=True
                )
            return 0

        lax.fori_loop(0, slots // chunk, body, 0)

    def relax(f, step, x, y, n, first, second):
        lane = lax.broadcasted_iota(jnp.int32, (n, LANES), 1)
        row = y + PAD

        def field(x, h, row):
            if step == 0:
                return rim[f * planes + x, h, pl.ds(row, n), :]
            return u[(step - 1) % 2, x, h, pl.ds(row, n), :]

        centre = [field(x, h, row) for h in range(2)]
        before, after = z_sides(centre[0], centre[1], lane)
        for h in range(2):
            at = (x - 1, h, pl.ds(y, n), slice(None))
            sides = axl[at] * field(x - 1, h, row) + axh[at] * field(x + 1, h, row)
            sides += ayl[at] * field(x, h, row - 1) + ayh[at] * field(x, h, row + 1)
            sides += azl[at] * before[h] + azh[at] * after[h]
            if step == 0:
                now = centre[h] * (1.0 / THETA)
                update = first * now + second * (centre[h] + (sides - centre[h]) * (1.0 / THETA))
            else:
                now = centre[h]
                update = first * d[at] + second * (rim[f * planes + x, h, pl.ds(row, n), :] + sides - now)
            d[at] = update
            u[step % 2, x, h, pl.ds(row, n), :] = now + update

    def pressure(f):
        rim_wait(f, (False,))
        factors = sweep_factors()

        def step_planes(step, start, count):
            low, high = (0, size_y + 2 * PAD) if step < CHEB - 2 else (PAD, size_y + PAD)
            n = (high - low) // 2
            for x in range(count):
                for y in (low, low + n):
                    relax(f, step, start + x, y, n, *factors[step])

        for step in range(CHEB - 1):
            step_planes(step, DEPTH + step + 1, size_x - 2 * (step + 1))
        rim_wait(f, (True,))
        for step in range(CHEB - 1):

            def body(side, _):
                step_planes(step, step + 1 + side * (planes - DEPTH - 2 * (step + 1)), DEPTH)
                return 0

            lax.fori_loop(0, 2, body, 0)
        return (CHEB - 2) % 2

    spread_grid(1, slot_sw * slot_rhs)
    sample_grid(pressure(1))
    got_1 = picked[...]
    slot_a = slot_steady * slot_rhs + slot_sw * got_1
    sum_a(pack_row([total(slot_rhs * slot_rhs), total(slot_rhs * slot_a)]))
    spread_grid(2, slot_sw * slot_a)
    sum_b()
    end = pressure(2)
    sum_bb, sum_ab = unpack_row(sum_c(), 2)
    sample_grid(end)
    got_2 = picked[...]
    start = jnp.sqrt(sum_bb + EPS)
    scale = 1.0 / start
    h_11 = sum_ab * scale * scale

    def basis(first, image, image_of_image):
        v_1 = first * scale
        w_1 = image * scale
        return v_1, w_1, w_1 - h_11 * v_1, image_of_image * scale - h_11 * w_1

    v_1, _, z, s_z = basis(slot_rhs, slot_a, slot_steady * slot_a + slot_sw * got_2)
    pairs = ((z, z), (s_z, v_1), (s_z, z), (s_z, s_z), (v_1, v_1), (v_1, z))
    back_a(got_1, got_2, pack_row([total(p * q) for p, q in pairs]))
    back_b()
    got_1, got_2, sums = back_c()
    image_1 = steady * rhs + sw * got_1
    v_1, w_1, z, s_z = basis(rhs, image_1, jnp.where(live, steady, 0.0) * image_1 + sw * got_2)
    zz, szv, szz, szsz, v1v1, v1z = unpack_row(sums, 6)
    h_21 = jnp.sqrt(zz + EPS)
    inverse = 1.0 / h_21
    v_2 = z * inverse
    w_2 = s_z * inverse
    w2v1, w2v2, w2w2 = szv * inverse, szz * inverse * inverse, szsz * inverse * inverse
    v1v2, v2v2 = v1z * inverse, zz * inverse * inverse
    h_12 = w2v1
    h_22 = w2v2 - h_12 * v1v2
    square = (
        w2w2
        + h_12 * h_12 * v1v1
        + h_22 * h_22 * v2v2
        - 2.0 * h_12 * w2v1
        - 2.0 * h_22 * w2v2
        + 2.0 * h_12 * h_22 * v1v2
    )
    h_32 = jnp.sqrt(jnp.maximum(square, 0.0) + EPS)
    y_1, y_2 = least_squares(start, [[h_11, h_21], [h_12, h_22, h_32]])
    sol[...] = y_1 * v_1 + y_2 * v_2
    res[...] = rhs - y_1 * w_1 - y_2 * w_2

    for f in range(3):
        rim_wait_sent(f)
    wait_for(fa_send.at[pl.ds(1, n_gy - 1)], a_ss.at[0])
    wait_for(ra_recv.at[pl.ds(1, n_gy - 1)], a_ss.at[1])
    wait_for(fb_send.at[pl.ds(1, n_gx - 1)], b_ss.at[0])
    wait_for(rb_send.at[pl.ds(1, n_gx - 1)], b_ss.at[1])
    wait_for(pb_recv.at[pl.ds(1, n_gx - 1)], p_ss.at[0])
    wait_for(pa_recv.at[pl.ds(1, n_gy - 1)], p_ss.at[1])


def on_device(n_gx, n_gy, beta, jump, stiff, weight, owner, cell, count):
    size_x, size_y, size_z = beta.shape
    points = jump.shape[0]
    rows = points // LANES
    owners = n_gx * n_gy
    columns = size_x * size_y
    planes = size_x + 2 * DEPTH
    wide = (planes, 2, size_y + 4 * PAD, LANES)
    tile = (planes - 2, 2, size_y + 2 * PAD, LANES)
    slots = n_gx * LANES
    dma = pltpu.SemaphoreType.DMA
    scratch = [
        pltpu.VMEM((owners, points), BF16),
        pltpu.VMEM((LANES, points), BF16),
        pltpu.VMEM((rows, LANES), jnp.int32),
        pltpu.VMEM((rows, LANES), jnp.int32),
        pltpu.VMEM((3 * planes,) + wide[1:], F32),
        pltpu.VMEM((2,) + wide, F32),
        pltpu.VMEM(tile, F32),
        pltpu.VMEM(tile, F32),
        pltpu.VMEM(tile, F32),
        pltpu.VMEM(tile, F32),
        pltpu.VMEM(tile, F32),
        pltpu.VMEM(tile, F32),
        pltpu.VMEM(tile, F32),
        pltpu.VMEM(tile, F32),
        pltpu.VMEM((columns, size_z), F32),
        pltpu.VMEM((2 * size_z, columns), BF16),
        pltpu.VMEM((columns, slots), BF16),
        pltpu.VMEM((2 * size_z, slots), BF16),
        pltpu.VMEM((n_gx, LANES), jnp.int32),
        pltpu.VMEM((n_gx, LANES), jnp.int32),
        pltpu.VMEM((n_gx, LANES), F32),
        pltpu.VMEM((2, rows, LANES), F32),
        pltpu.VMEM((n_gy, 4 * n_gx, LANES), F32),
        pltpu.VMEM((n_gy, 4 * n_gx, LANES), F32),
        pltpu.VMEM((n_gx, 4, LANES), F32),
        pltpu.VMEM((n_gx, 4, LANES), F32),
        pltpu.VMEM((n_gx, 4, LANES), F32),
        pltpu.VMEM((n_gx, 4, LANES), F32),
        pltpu.VMEM((2 * n_gx + PAD, LANES), F32),
        pltpu.VMEM((n_gy, 2 * n_gx + PAD, LANES), F32),
        pltpu.VMEM((2, LANES), F32),
        pltpu.VMEM((n_gx, 2, LANES), F32),
        pltpu.VMEM((2, LANES), F32),
        pltpu.VMEM((n_gy, 2, LANES), F32),
    ] + [dma((2,))] * 6 + [dma((3, len(SIDES)))] * 2
    vmem = pl.BlockSpec(memory_space=pltpu.VMEM)
    out = jax.ShapeDtypeStruct((rows, LANES), F32)
    solution, residual = pl.pallas_call(
        functools.partial(kernel, n_gx, n_gy),
        out_shape=(out, out),
        in_specs=[vmem] * 7,
        out_specs=(vmem, vmem),
        scratch_shapes=scratch,
        compiler_params=pltpu.CompilerParams(
            collective_id=0, has_side_effects=True, vmem_limit_bytes=56 * 1024 * 1024
        ),
    )(
        beta,
        jump.reshape(rows, LANES),
        stiff.reshape(rows, LANES),
        weight.reshape(rows, LANES),
        owner.reshape(rows, LANES),
        cell.reshape(rows, LANES),
        count.reshape(1, 1),
    )
    return solution.reshape(points), residual.reshape(points)


def solution(mesh):
    points = P(("gx", "gy"))
    return jax.shard_map(
        functools.partial(on_device, mesh.shape["gx"], mesh.shape["gy"]),
        mesh=mesh,
        in_specs=(P("gx", "gy", None), points, points, points, P(("gx", "gy"), None), points, points),
        out_specs=(points, points),
        check_vma=False,
    )
```
